128 devices in a mesh: gx: 8 (over z, core), yz: 16 (over y, x).
Axes of the slice: x: 4, y: 4, z: 4, core: 2. Of those that a mesh axis runs over, the one named last changes fastest.
Arguments:
- tokens: bfloat16 [2, 256, 10240], P(None, 'gx', 'yz'), may hold values from -16 to 16
- norm_gain: float32 [10240], P('yz'), may hold values from 0.5 to 1.5
- w_query: bfloat16 [10240, 12288], P('yz', 'gx'), may hold values from -0.0625 to 0.0625
- w_shared: bfloat16 [10240, 512], P('yz'), may hold values from -0.0625 to 0.0625
- w_gate: bfloat16 [10240, 36864], P('yz', 'gx'), may hold values from -0.0625 to 0.0625
- w_up: bfloat16 [10240, 36864], P('yz', 'gx'), may hold values from -0.0625 to 0.0625
- w_out: bfloat16 [12288, 10240], P('gx', 'yz'), may hold values from -0.0546875 to 0.0546875
- w_down: bfloat16 [36864, 10240], P('gx', 'yz'), may hold values from -0.03125 to 0.03125
- key_cache: bfloat16 [256, 2048, 256], P(('gx', 'yz')), may hold values from -512 to 512
- value_cache: bfloat16 [256, 2048, 256], P(('gx', 'yz')), may hold values from -12 to 12
- lengths: int32 [256], P(('gx', 'yz')), may hold values from 1 to 2048, as said below
Outputs:
- layer_out: bfloat16 [2, 256, 10240], P(None, 'gx', 'yz')
- new_entries: bfloat16 [2, 256, 512], P(None, ('gx', 'yz'))
The draws below stay inside these ranges and needn't reach their ends.
Inputs may be any that keep to these rules, and one draw needn't show every extreme that they name: Row r's caches hold live entries in their first lengths[r] slots; at least one row's cache is full.
All inputs are finite; a program needn't handle non-finite values.
Results may differ from the reference program's by a relative error of at most 0.0084.
Values may be sent and summed in bfloat16 or wider, within the bound.
A program may use at most 192 MiB of HBM per device.

```python
import math
import jax
import jax.numpy as jnp
from jax import lax

D = 10240
HEADS = 48
HEAD_DIM = 256
FF = 36864
CTX = 2048
STEPS = 2
ROWS = 256


def draw_tokens(key, part):
    first_key = jax.random.fold_in(jax.random.fold_in(key, 11), 0)
    column = jnp.arange(D, dtype=jnp.float32) / D
    values = jnp.clip(jax.random.normal(first_key, (STEPS, ROWS, D), jnp.float32), -6.0, 6.0)
    result = values * 0.6 * jnp.exp(column * math.log(3.0))
    return result.astype(jnp.bfloat16)


def draw_key_cache(key, part):
    keys = jax.random.split(jax.random.fold_in(key, 23), 1)
    result = jnp.clip(jax.random.normal(keys[0], (ROWS, CTX, HEAD_DIM), jnp.float32), -6.0, 6.0) * 1.5
    return result.astype(jnp.bfloat16)


def draw_lengths(key, part):
    first_key, second_key = jax.random.split(jax.random.fold_in(key, 37), 2)
    drawn = jax.random.randint(first_key, (ROWS,), 1, CTX + 1)
    chosen = jax.random.randint(second_key, (), 0, ROWS)
    return jnp.where(jnp.arange(ROWS, dtype=jnp.int32) == chosen, CTX, drawn).astype(jnp.int32)


def steps_of(stream_key, dims, cuts, least, largest):
    factor_of = 1.0
    for dim, shards_of in cuts:
        heights = jax.random.uniform(jax.random.fold_in(jax.random.fold_in(stream_key, 6), dim), (shards_of,), jnp.float32, least / len(cuts), largest / len(cuts))
        factor_of = factor_of * jnp.repeat(jnp.exp(heights), dims[dim] // shards_of).reshape((-1,) + (1,) * (len(dims) - 1 - dim))
    return factor_of


def scatter_about(own_key, shape, width, most, shards=(), kind=jnp.bfloat16):
    values = jax.random.normal(own_key, shape, jnp.float32) * width
    if len(shards) > 0:
        values = steps_of(own_key, shape, shards, -0.22, 0.18) * values
    return jnp.clip(values, min=-most, max=most).astype(kind)


def setup_inputs(seed: int = 0) -> dict:
    splits = jax.random.split(jax.random.key(seed), 12)
    return {
        "tokens": draw_tokens(jax.random.fold_in(splits[11], 71), 0),
        "norm_gain": jnp.clip(1.0 + 0.1 * jax.random.normal(splits[1], (D,), jnp.float32), 0.5, 1.5),
        "w_query": scatter_about(splits[2], (D, HEADS * HEAD_DIM), D ** -0.5, 0.0625, ((0, 16), (1, 8))),
        "w_shared": scatter_about(splits[3], (D, 2 * HEAD_DIM), D ** -0.5, 0.0625, ((0, 16),)),
        "w_gate": scatter_about(splits[4], (D, FF), D ** -0.5, 0.0625, ((0, 16), (1, 8))),
        "w_up": scatter_about(splits[5], (D, FF), D ** -0.5, 0.0625, ((0, 16), (1, 8))),
        "w_out": scatter_about(splits[6], (HEADS * HEAD_DIM, D), (HEADS * HEAD_DIM) ** -0.5, 0.0546875, ((0, 8), (1, 16))),
        "w_down": scatter_about(splits[7], (FF, D), FF ** -0.5, 0.03125, ((0, 8), (1, 16))),
        "key_cache": draw_key_cache(jax.random.fold_in(splits[11], 71), 0),
        "value_cache": scatter_about(splits[9], (ROWS, CTX, HEAD_DIM), 2.0, 12.0, ((0, 128),)),
        "lengths": draw_lengths(jax.random.fold_in(splits[11], 71), 0),
    }


EPSILON = 1e-06

def rotate_pairs(vectors, positions):
    half_dim = vectors.shape[-1] // 2
    frequency = jnp.exp(jnp.arange(half_dim, dtype=jnp.float32) * (-2.0 * math.log(10000.0) / vectors.shape[-1]))
    angles = positions[:, None, None] * frequency
    cosine = jnp.cos(angles)
    sine_part = jnp.sin(angles)
    front_part = vectors[..., :half_dim]
    back_part = vectors[..., half_dim:]
    return jnp.concatenate([front_part * cosine - back_part * sine_part, back_part * cosine + front_part * sine_part], axis=-1)

def attend_rows(query_heads, key_cache, value_cache, lengths, new_keys, new_values):
    head_dim = query_heads.shape[-1]
    factor = 1.0 / math.sqrt(head_dim)
    query_wide = query_heads.astype(jnp.float32)
    cached = jnp.einsum('rhd,rcd->rhc', query_wide, key_cache.astype(jnp.float32)) * factor
    slot_index = jnp.arange(key_cache.shape[1], dtype=jnp.int32)
    live_mask = slot_index[None, None, :] < lengths[:, None, None]
    cached = jnp.where(live_mask, cached, -jnp.inf)
    fresh_scores = jnp.einsum('rhd,rnd->rhn', query_wide, new_keys.astype(jnp.float32)) * factor
    row_top = jnp.maximum(lax.optimization_barrier(jnp.max(cached, axis=2)), lax.optimization_barrier(jnp.max(fresh_scores, axis=2)))[:, :, None]
    cached_exp = jnp.exp(cached - row_top)
    fresh_exp = jnp.exp(fresh_scores - row_top)
    denominator = lax.optimization_barrier(jnp.sum(cached_exp, axis=2, keepdims=True)) + lax.optimization_barrier(jnp.sum(fresh_exp, axis=2, keepdims=True))
    cached_weight = (cached_exp / denominator).astype(jnp.bfloat16)
    fresh_weight = (fresh_exp / denominator).astype(jnp.bfloat16)
    attended = jnp.einsum('rhc,rcd->rhd', cached_weight.astype(jnp.float32), value_cache.astype(jnp.float32))
    attended = attended + jnp.einsum('rhn,rnd->rhd', fresh_weight.astype(jnp.float32), new_values.astype(jnp.float32))
    return attended.astype(jnp.bfloat16)

def reference(tokens, norm_gain, w_query, w_shared, w_gate, w_up, w_out, w_down, key_cache, value_cache, lengths):
    gain_row = norm_gain.astype(jnp.float32)
    query_width = HEADS * HEAD_DIM
    fresh_keys = []
    fresh_values = []
    outputs = []
    entries = []
    for step_index in range(STEPS):
        current_float = tokens[step_index].astype(jnp.float32)
        square_total = lax.optimization_barrier(jnp.sum(current_float * current_float, axis=1))
        inverse_rms = lax.rsqrt(square_total / D + EPSILON)
        normed = (current_float * inverse_rms[:, None] * gain_row).astype(jnp.bfloat16)
        query_sum = jnp.dot(normed, w_query, preferred_element_type=jnp.float32)
        gate_sum = jnp.dot(normed, w_gate, preferred_element_type=jnp.float32)
        up_sum = jnp.dot(normed, w_up, preferred_element_type=jnp.float32)
        shared_sum = jnp.dot(normed, w_shared, preferred_element_type=jnp.float32)
        positions = (lengths + step_index).astype(jnp.float32)
        query_round = lax.optimization_barrier(query_sum.astype(jnp.bfloat16)).astype(jnp.float32)
        query_heads = rotate_pairs(query_round.reshape(ROWS, HEADS, HEAD_DIM), positions).astype(jnp.bfloat16)
        key_round = lax.optimization_barrier(shared_sum[:, :HEAD_DIM].astype(jnp.bfloat16)).astype(jnp.float32)
        key_now = rotate_pairs(key_round[:, None, :], positions)[:, 0, :].astype(jnp.bfloat16)
        value_now = shared_sum[:, HEAD_DIM:].astype(jnp.bfloat16)
        fresh_keys.append(key_now)
        fresh_values.append(value_now)
        new_keys = jnp.stack(fresh_keys, axis=1)
        new_values = jnp.stack(fresh_values, axis=1)
        attended = attend_rows(query_heads, key_cache, value_cache, lengths, new_keys, new_values).reshape(ROWS, query_width)
        hidden = (jax.nn.silu(gate_sum) * up_sum).astype(jnp.bfloat16)
        branch_sum = jnp.dot(attended, w_out, preferred_element_type=jnp.float32) + jnp.dot(hidden, w_down, preferred_element_type=jnp.float32)
        outputs.append((current_float + branch_sum).astype(jnp.bfloat16))
        entries.append(jnp.concatenate([key_now, value_now], axis=1))
    return (jnp.stack(outputs), jnp.stack(entries))
```

```python
import functools
import math

import jax
import jax.numpy as jnp
from jax import lax
from jax.experimental import pallas as pl
from jax.experimental.pallas import tpu as pltpu
from jax.sharding import PartitionSpec as P

EPSILON = 1e-06
MESH = pl.DeviceIdType.MESH
BF = jnp.bfloat16
F32 = jnp.float32
HIDDEN_CHUNKS = (768, 768, 768)
RING = 4


def dot(a, b):
    return jnp.dot(a, b, preferred_element_type=F32)


def dot_t(a, b):
    return lax.dot_general(a, b, (((1,), (1,)), ((), ())), preferred_element_type=F32)


def iota(shape, dim):
    return lax.broadcasted_iota(jnp.int32, shape, dim)


def one_hot(mask):
    return jnp.where(mask, 1.0, 0.0).astype(BF)


def add_f32(*terms):
    total = terms[0].astype(F32)
    for term in terms[1:]:
        total = total + term.astype(F32)
    return total


class Scratch:
    def __init__(self):
        self.names, self.shapes = [], []

    def add(self, name, shape, dtype=BF):
        self.names.append(name)
        self.shapes.append(pltpu.VMEM(shape, dtype))


def query_width(f):
    return 768 + 128 * f


def scratch_plan(columns):
    s = Scratch()
    for f in range(2):
        for k in range(1 + len(HIDDEN_CHUNKS)):
            hc = 768 if k == 0 else HIDDEN_CHUNKS[k - 1]
            w = query_width(f) if k == 0 else 2 * hc
            t = (k, f)
            s.add(("w1",) + t, (columns, w))
            s.add(("part",) + t, (4, 4, 32, w))
            s.add(("r1",) + t, (2, 2, 32, w))
            s.add(("r2",) + t, (2, 4, 32, w))
            s.add(("q1",) + t, (2, 16, w))
            s.add(("q2",) + t, (2, 32, w))
            s.add(("ag",) + t, (4, 4, 32, hc))
            s.add(("w2",) + t, (hc, columns))
    s.add("keys", (2, 2048, 256))
    s.add("values", (2, 2048, 256))
    s.add("tk", (8, 64, columns))
    s.add("xs", (2, 512, columns))
    s.add("acc", (512, columns), F32)
    s.add("ob", (2, 4, 64, columns))
    s.add("fr", (4, 64, columns))
    s.add("fz1", (2, 32, columns))
    s.add("fz2", (2, 64, columns))
    s.add("qsend", (8, 32, 256))
    s.add("qrecv", (8, 32, 256))
    s.add("asend", (8, 32, 256))
    s.add("arecv", (8, 32, 256))
    s.add("inv", (32, 128), F32)
    return s


class Half:
    pass


def kernel(
    plan_names,
    model_width,
    tok,
    gain,
    wq,
    wsh,
    wg,
    wu,
    wo,
    wd,
    kc,
    vc,
    lens,
    cos_ref,
    sin_ref,
    out,
    entries,
    *scratch,
):
    n = len(plan_names)
    b = dict(zip(plan_names, scratch[:n]))
    send_sem, recv_sem, local_sem = scratch[n:]
    columns = tok.shape[1]
    g = lax.axis_index("gx")
    q = lax.axis_index("yz")
    z, c = g // 2, lax.rem(g, 2)
    y, x = q // 4, lax.rem(q, 4)

    def step(v, d):
        return lax.rem(v + d + RING, RING)

    def at_x(d):
        return (g, y * 4 + step(x, d))

    def at_y(d):
        return (g, step(y, d) * 4 + x)

    def at_z(d):
        return (step(z, d) * 2 + c, q)

    partner = (z * 2 + 1 - c, q)

    started = []

    def rc(src, dst, dev):
        i = len(started)
        cp = pltpu.make_async_remote_copy(
            src_ref=src,
            dst_ref=dst,
            send_sem=send_sem.at[i],
            recv_sem=recv_sem.at[i],
            device_id=dev,
            device_id_type=MESH,
        )
        cp.start()
        started.append(cp)
        return cp

    loads = {}

    def load(name, src, dst):
        i = sum(len(v) for v in loads.values())
        cp = pltpu.make_async_copy(src, dst, local_sem.at[i])
        cp.start()
        loads.setdefault(name, []).append(cp)

    def loaded(name):
        for cp in loads[name]:
            cp.wait()

    load("tok", tok, b["tk"].at[g])
    shared_at = pl.multiple_of(z * 128, 128)
    load(("w1", 0, 1), wq.at[:, 768:1536], b["w1", 0, 1].at[:, 0:768])
    load(("w1", 0, 1), wsh.at[:, pl.ds(shared_at, 128)], b["w1", 0, 1].at[:, 768:896])
    load(("w1", 0, 0), wq.at[:, 0:768], b["w1", 0, 0])
    hidden_at = {}
    base = 0
    for k, hc in enumerate(HIDDEN_CHUNKS, 1):
        for f in range(2):
            hidden_at[k, f] = base
            base += hc

    def load_w1(k):
        hc = HIDDEN_CHUNKS[k - 1]
        for f in range(2):
            at = hidden_at[k, f]
            load(("w1", k, f), wg.at[:, at : at + hc], b["w1", k, f].at[:, 0:hc])
            load(("w1", k, f), wu.at[:, at : at + hc], b["w1", k, f].at[:, hc : 2 * hc])

    barrier = pltpu.get_barrier_semaphore()
    others = [lax.rem(g + d, 8) for d in range(1, 8)]
    peers = [at_x(1), at_x(-1), at_y(1), at_y(-1)] + [(o, q) for o in others]
    for peer in peers:
        pl.semaphore_signal(barrier, inc=1, device_id=peer, device_id_type=MESH)
    loaded("tok")
    pl.semaphore_wait(barrier, len(peers))

    tk = b["tk"]

    def block(zz):
        return zz * 2 + c

    zr, zl, zo = step(z, 1), step(z, -1), step(z, 2)
    own = tk.at[g]
    t_r = rc(own, own, at_z(1))
    t_l = rc(own, own, at_z(-1))
    pairs = [rc(own, own, partner)]
    for k in range(1, 1 + len(HIDDEN_CHUNKS)):
        load_w1(k)
    t_r.wait_recv()
    blk = tk.at[block(zl), 0:32]
    f_r = rc(blk, blk, at_z(1))
    blk = tk.at[block(zl)]
    pairs.append(rc(blk, blk, partner))
    t_l.wait_recv()
    blk = tk.at[block(zr), 32:64]
    f_l = rc(blk, blk, at_z(-1))
    blk = tk.at[block(zr)]
    pairs.append(rc(blk, blk, partner))
    f_r.wait_recv()
    f_l.wait_recv()
    blk = tk.at[block(zo)]
    pairs.append(rc(blk, blk, partner))
    for k in range(1 + len(HIDDEN_CHUNKS)):
        for f in range(2):
            if k == 0:
                load(("w2", k, f), wo.at[768 * f : 768 * f + 768], b["w2", k, f])
            else:
                at = hidden_at[k, f]
                load(("w2", k, f), wd.at[at : at + HIDDEN_CHUNKS[k - 1]], b["w2", k, f])
    load("kv", kc, b["keys"])
    load("kv", vc, b["values"])
    for cp in pairs:
        cp.wait_recv()

    tokens_all = tk[...].reshape(512, columns)
    row_i, col_i = iota((512, 512), 0), iota((512, 512), 1)
    tail = (((row_i >> 2) & 7) << 6) | (((row_i >> 1) & 1) << 5) | (row_i & 1)
    d1, d2 = (row_i >> 7) & 3, (row_i >> 5) & 3
    source = {0: tail | (d2 << 3) | (d1 << 1), 1: tail | (d1 << 3) | (d2 << 1)}
    squares = None
    gain_row = gain[...]
    for f in (1, 0):
        rows = dot(one_hot(source[f] == col_i), tokens_all)
        if f == 1:
            squares = jnp.sum(rows * rows, axis=1, keepdims=True)
        b["xs"][f] = (rows * gain_row).astype(BF)

    lane = iota((1, 128), 1)
    mine = (lane >> 6) == c
    spread = 1.0 + (lane & 63).astype(F32) * (1.0 / 64.0)

    halves = {}
    for f in range(2):
        h = Half()
        first, second = (at_x, at_y) if f == 0 else (at_y, at_x)
        p1, p2 = (x, y) if f == 0 else (y, x)
        h.first, h.second, h.p1, h.p2 = first, second, p1, p2
        h.r1, h.l1, h.o1 = step(p1, 1), step(p1, -1), step(p1, 2)
        h.r2, h.l2, h.o2 = step(p2, 1), step(p2, -1), step(p2, 2)
        halves[f] = h
    cps = {}

    def product(k, f):
        loaded(("w1", k, f))
        part, w1 = b["part", k, f], b["w1", k, f]
        w = 768 if k == 0 else w1.shape[1]

        @pl.loop(0, w // 256)
        def _(i):
            at = pl.ds(pl.multiple_of(i * 256, 256), 256)
            value = dot(b["xs"][f], w1[:, at]).astype(BF)
            part[:, :, :, at] = value.reshape(4, 4, 32, 256)

        if k == 0 and f == 1:
            value = dot(b["xs"][f], w1[:, 768:896])
            value = jnp.where(mine, value, squares * spread).astype(BF)
            part[:, :, :, 768:896] = value.reshape(4, 4, 32, 128)

    def s1(k, f):
        h, part, r1, r2 = halves[f], b["part", k, f], b["r1", k, f], b["r2", k, f]
        cps[k, f] = [
            rc(part.at[h.o1, 0:2], r1.at[0], h.first(1)),
            rc(part.at[h.o1, 2:4], r1.at[1], h.first(-1)),
            rc(part.at[h.r1, 2:4], r2.at[0, 2:4], h.first(1)),
            rc(part.at[h.l1, 0:2], r2.at[1, 0:2], h.first(-1)),
        ]

    def s2(k, f):
        h, part, r1, r2 = halves[f], b["part", k, f], b["r1", k, f], b["r2", k, f]
        one, two, three, four = cps[k, f]
        one.wait_recv()
        part[h.r1, 0:2] = add_f32(part[h.r1, 0:2], r1[0]).astype(BF)
        five = rc(part.at[h.r1, 0:2], r2.at[0, 0:2], h.first(1))
        two.wait_recv()
        part[h.l1, 2:4] = add_f32(part[h.l1, 2:4], r1[1]).astype(BF)
        six = rc(part.at[h.l1, 2:4], r2.at[1, 2:4], h.first(-1))
        cps[k, f] = [three, four, five, six]

    def s3(k, f):
        h, part, r2 = halves[f], b["part", k, f], b["r2", k, f]
        q1, q2 = b["q1", k, f], b["q2", k, f]
        for cp in cps[k, f]:
            cp.wait_recv()

        def total(d):
            part[h.p1, d] = add_f32(part[h.p1, d], r2[0, d], r2[1, d]).astype(BF)

        total(h.o2)
        new = [
            rc(part.at[h.p1, h.o2, 0:16], q1.at[0], h.second(1)),
            rc(part.at[h.p1, h.o2, 16:32], q1.at[1], h.second(-1)),
        ]
        total(h.r2)
        new.append(rc(part.at[h.p1, h.r2, 16:32], q2.at[0, 16:32], h.second(1)))
        total(h.l2)
        new.append(rc(part.at[h.p1, h.l2, 0:16], q2.at[1, 0:16], h.second(-1)))
        total(h.p2)
        cps[k, f] = new

    def s4(k, f):
        h, part = halves[f], b["part", k, f]
        q1, q2 = b["q1", k, f], b["q2", k, f]
        one, two, three, four = cps[k, f]
        one.wait_recv()
        part[h.p1, h.r2, 0:16] = add_f32(part[h.p1, h.r2, 0:16], q1[0]).astype(BF)
        five = rc(part.at[h.p1, h.r2, 0:16], q2.at[0, 0:16], h.second(1))
        two.wait_recv()
        part[h.p1, h.l2, 16:32] = add_f32(part[h.p1, h.l2, 16:32], q1[1]).astype(BF)
        six = rc(part.at[h.p1, h.l2, 16:32], q2.at[1, 16:32], h.second(-1))
        cps[k, f] = [three, four, five, six]

    def s5(k, f, lo, hi):
        h, part, q2 = halves[f], b["part", k, f], b["q2", k, f]
        return add_f32(part[h.p1, h.p2, :, lo:hi], q2[0, :, lo:hi], q2[1, :, lo:hi])

    def s5_wait(k, f):
        for cp in cps[k, f]:
            cp.wait_recv()

    def hidden(k, f):
        s5_wait(k, f)
        h, hc = halves[f], HIDDEN_CHUNKS[k - 1]
        inv = b["inv"][:, 0:1]
        gate = s5(k, f, 0, hc) * inv
        up = s5(k, f, hc, 2 * hc) * inv
        value = gate * (1.0 / (1.0 + jnp.exp(-gate))) * up
        b["ag", k, f][h.p2, h.p1] = value.astype(BF)

    def g1(k, f):
        h, ag = halves[f], b["ag", k, f]
        blk = ag.at[h.p2, h.p1]
        cps["g", k, f] = [rc(blk, blk, h.first(1)), rc(blk, blk, h.first(-1))]

    def g2(k, f):
        h, ag = halves[f], b["ag", k, f]
        one, two = cps["g", k, f]
        one.wait_recv()
        blk = ag.at[h.p2, h.l1, 0:16]
        three = rc(blk, blk, h.first(1))
        two.wait_recv()
        blk = ag.at[h.p2, h.r1, 16:32]
        four = rc(blk, blk, h.first(-1))
        cps["g", k, f] = [three, four]

    def g3(k, f):
        h, ag = halves[f], b["ag", k, f]
        for cp in cps["g", k, f]:
            cp.wait_recv()
        blk = ag.at[h.p2]
        cps["g", k, f] = [rc(blk, blk, h.second(1)), rc(blk, blk, h.second(-1))]

    def g4(k, f):
        h, ag = halves[f], b["ag", k, f]
        one, two = cps["g", k, f]
        one.wait_recv()
        blk = ag.at[h.l2, 0:2]
        three = rc(blk, blk, h.second(1))
        two.wait_recv()
        blk = ag.at[h.r2, 2:4]
        four = rc(blk, blk, h.second(-1))
        cps["g", k, f] = [three, four]

    first_product = [True]

    def second(k, f):
        for cp in cps["g", k, f]:
            cp.wait_recv()
        loaded(("w2", k, f))
        ag, w2, acc = b["ag", k, f], b["w2", k, f], b["acc"]
        start = first_product[0]
        first_product[0] = False
        for lo, hi in ((0, 256), (256, 512), (512, columns)):
            value = dot(ag[...].reshape(512, ag.shape[3]), w2[:, lo:hi])
            if start:
                acc[:, lo:hi] = value
            elif f == 0:
                acc[:, lo:hi] += value
            else:
                for yy in range(4):
                    for xx in range(4):
                        to, frm = (yy * 4 + xx) * 32, (xx * 4 + yy) * 32
                        acc[to : to + 32, lo:hi] += value[frm : frm + 32]

    def exchange(send, recv):
        done = []
        for o in others:
            done.append(rc(send.at[o], recv.at[g], (o, q)))
        recv[g] = send[g]
        return done

    def spread_rows(head):
        row, col = iota((256, 32), 0), iota((256, 32), 1)
        return one_hot((col == (((row >> 5) << 2) | (row & 3))) & (((row >> 2) & 7) == head))

    def collect_rows(head):
        row, col = iota((32, 256), 0), iota((32, 256), 1)
        return one_hot((row == (((col >> 5) << 2) | (col & 3))) & (((col >> 2) & 7) == head))

    def query_out():
        s5_wait(0, 0)
        s5_wait(0, 1)
        shared = s5(0, 1, 768, 896)
        total = jnp.sum(jnp.where(mine, 0.0, shared), axis=1, keepdims=True) * (1.0 / 95.5)
        inv = lax.rsqrt(total / model_width + EPSILON)
        b["inv"][...] = jnp.broadcast_to(inv, (32, 128))
        shared = jnp.where(mine, shared * inv, 0.0)
        low = lax.rem(z, 2) == 0
        shared = jnp.concatenate([jnp.where(low, shared, 0.0), jnp.where(low, 0.0, shared)], axis=1)
        rows = dot(spread_rows(6), shared.astype(BF))
        for f in range(2):
            for i in range(3):
                piece = (s5(0, f, i * 256, i * 256 + 256) * inv).astype(BF)
                rows = rows + dot(spread_rows(f * 3 + i), piece)
        b["qsend"][...] = rows.astype(BF).reshape(8, 32, 256)
        cps["q"] = exchange(b["qsend"], b["qrecv"])

    def rotate(rows):
        count = rows.shape[0]
        rows = rows.reshape(count // 8, 8, 256)
        front, back = rows[:, :, :128], rows[:, :, 128:]
        cosine, sine = cos_ref[...][None], sin_ref[...][None]
        return jnp.concatenate(
            [front * cosine - back * sine, back * cosine + front * sine], axis=2
        ).reshape(count, 256)

    def attention():
        for cp in cps["q"]:
            cp.wait_recv()
        loaded("kv")
        raw = b["qrecv"][...].reshape(256, 256)
        queries = rotate(raw.astype(F32)).astype(BF)
        row, col = iota((128, 256), 0), iota((128, 256), 1)
        pick = (row < 4) & ((col & 31) == row + 24)
        key_now = rotate(dot(one_hot(pick & (col < 128)), raw)).astype(BF)
        value_now = dot(one_hot(pick & (col >= 128)), raw).astype(BF)
        fresh = jnp.concatenate([key_now[0:8], value_now[0:8]], axis=1)
        entries[...] = fresh
        result = None
        for j in range(2):
            chosen = one_hot(col == (((row >> 4) << 5) + ((row & 15) << 1) + j))
            heads = dot(chosen, queries).astype(BF)
            scores = dot_t(heads, b["keys"][j]) * (1.0 / 16.0)
            live = iota(scores.shape, 1) < lens[j]
            scores = jnp.where(live, scores, -jnp.inf)
            now = dot_t(heads, key_now) * (1.0 / 16.0)
            r, n_ = iota((128, 128), 0), iota((128, 128), 1)
            now = jnp.where((n_ < 4) & ((n_ & 1) == j) & ((n_ >> 1) <= (r & 1)), now, -jnp.inf)
            top = jnp.maximum(
                jnp.max(scores, axis=1, keepdims=True), jnp.max(now, axis=1, keepdims=True)
            )
            scores = jnp.exp(scores - top)
            now = jnp.exp(now - top)
            under = jnp.sum(scores, axis=1, keepdims=True) + jnp.sum(now, axis=1, keepdims=True)
            scale = 1.0 / under
            mixed = dot((scores * scale).astype(BF), b["values"][j]) + dot(
                (now * scale).astype(BF), value_now
            )
            brow, bcol = iota((256, 128), 0), iota((256, 128), 1)
            back = one_hot(brow == (((bcol >> 4) << 5) + ((bcol & 15) << 1) + j))
            term = dot(back, mixed.astype(BF))
            result = term if result is None else result + term
        b["asend"][...] = result.astype(BF).reshape(8, 32, 256)
        cps["a"] = exchange(b["asend"], b["arecv"])

    def attended():
        for cp in cps["a"]:
            cp.wait_recv()
        raw = b["arecv"][...].reshape(256, 256)
        for f in range(2):
            h = halves[f]
            for i in range(3):
                value = dot(collect_rows(f * 3 + i), raw).astype(BF)
                b["ag", 0, f][h.p2, h.p1, :, i * 256 : i * 256 + 256] = value

    def both(stage, k):
        for f in (1, 0) if k == 0 else (0, 1):
            stage(k, f)

    def start(k):
        for f in (1, 0) if k == 0 else (0, 1):
            product(k, f)
            s1(k, f)

    start(0)
    start(1)
    both(s2, 0)
    both(s3, 0)
    both(s2, 1)
    both(s4, 0)
    start(2)
    both(s3, 1)
    query_out()
    both(s2, 2)
    both(s4, 1)
    start(3)
    attention()
    both(s3, 2)
    both(hidden, 1)
    both(g1, 1)
    both(s2, 3)
    both(s4, 2)
    attended()
    both(g1, 0)
    both(g2, 1)
    both(s3, 3)
    both(hidden, 2)
    both(g1, 2)
    both(g3, 1)
    both(g2, 0)
    both(s4, 3)
    both(g2, 2)
    both(g3, 0)
    both(g4, 1)
    both(hidden, 3)
    both(g1, 3)
    both(g3, 2)
    both(g4, 0)
    both(g2, 3)
    both(second, 1)
    both(g3, 3)
    both(g4, 2)
    both(second, 0)
    both(g4, 3)
    both(second, 2)
    both(second, 3)

    row_o, col_o = iota((512, 512), 0), iota((512, 512), 1)
    gx_o = (((row_o >> 6) & 3) << 1) | (row_o >> 8)
    wanted = (((row_o >> 1) & 15) << 5) | (gx_o << 2) | (((row_o >> 5) & 1) << 1) | (row_o & 1)
    moved = dot(one_hot(wanted == col_o), b["acc"][...].astype(BF)).astype(BF)
    ob, fr, fz1, fz2 = b["ob"], b["fr"], b["fz1"], b["fz2"]
    ob[...] = moved.reshape(2, 4, 64, columns)
    cp = rc(ob.at[1 - c], fr, partner)
    cp.wait_recv()

    def add_partner(zz):
        ob[c, zz] = add_f32(ob[c, zz], fr[zz]).astype(BF)

    add_partner(zo)
    one = rc(ob.at[c, zo, 0:32], fz1.at[0], at_z(1))
    two = rc(ob.at[c, zo, 32:64], fz1.at[1], at_z(-1))
    add_partner(zr)
    three = rc(ob.at[c, zr, 32:64], fz2.at[0, 32:64], at_z(1))
    add_partner(zl)
    four = rc(ob.at[c, zl, 0:32], fz2.at[1, 0:32], at_z(-1))
    one.wait_recv()
    ob[c, zr, 0:32] = add_f32(ob[c, zr, 0:32], fz1[0]).astype(BF)
    five = rc(ob.at[c, zr, 0:32], fz2.at[0, 0:32], at_z(1))
    two.wait_recv()
    ob[c, zl, 32:64] = add_f32(ob[c, zl, 32:64], fz1[1]).astype(BF)
    six = rc(ob.at[c, zl, 32:64], fz2.at[1, 32:64], at_z(-1))
    mine_sum = add_f32(b["tk"][g], ob[c, z], fr[z])
    for cp in (three, four, five, six):
        cp.wait_recv()
    out[...] = (mine_sum + fz2[0].astype(F32) + fz2[1].astype(F32)).astype(BF)
    for cp in started:
        cp.wait_send()


def local(
    tokens,
    norm_gain,
    w_query,
    w_shared,
    w_gate,
    w_up,
    w_out,
    w_down,
    key_cache,
    value_cache,
    lengths,
):
    steps, block_rows, columns = tokens.shape
    model_width = columns * lax.axis_size("yz")
    rows = jnp.arange(8)
    positions = (lengths[rows % 2] + (rows // 2) % 2).astype(F32)
    frequency = jnp.exp(jnp.arange(128, dtype=F32) * (-2.0 * math.log(10000.0) / 256))
    angles = positions[:, None] * frequency
    plan = scratch_plan(columns)
    hbm = pl.BlockSpec(memory_space=pl.ANY)
    vmem = pl.BlockSpec(memory_space=pltpu.VMEM)
    smem = pl.BlockSpec(memory_space=pltpu.SMEM)
    copies = 256
    layer, entries = pl.pallas_call(
        functools.partial(kernel, plan.names, model_width),
        out_shape=(
            jax.ShapeDtypeStruct((steps * block_rows, columns), BF),
            jax.ShapeDtypeStruct((8, 512), BF),
        ),
        in_specs=[hbm, vmem] + [hbm] * 8 + [smem, vmem, vmem],
        out_specs=(vmem, vmem),
        scratch_shapes=plan.shapes
        + [
            pltpu.SemaphoreType.DMA((copies,)),
            pltpu.SemaphoreType.DMA((copies,)),
            pltpu.SemaphoreType.DMA((48,)),
        ],
        compiler_params=pltpu.CompilerParams(
            collective_id=0, has_side_effects=True, vmem_limit_bytes=64 << 20
        ),
        cost_estimate=pl.CostEstimate(
            flops=12 * 10**9, bytes_accessed=28 * 10**6, transcendentals=10**6
        ),
    )(
        tokens.reshape(steps * block_rows, columns),
        norm_gain[None],
        w_query,
        w_shared,
        w_gate,
        w_up,
        w_out,
        w_down,
        key_cache,
        value_cache,
        lengths,
        jnp.cos(angles),
        jnp.sin(angles),
    )
    return layer.reshape(steps, block_rows, columns), entries[:4].reshape(2, 2, 512)


def solution(mesh):
    in_specs = (
        P(None, "gx", "yz"),
        P("yz"),
        P("yz", "gx"),
        P("yz", None),
        P("yz", "gx"),
        P("yz", "gx"),
        P("gx", "yz"),
        P("gx", "yz"),
        P(("gx", "yz"), None, None),
        P(("gx", "yz"), None, None),
        P(("gx", "yz")),
    )
    out_specs = (P(None, "gx", "yz"), P(None, ("gx", "yz"), None))
    return jax.shard_map(local, mesh=mesh, in_specs=in_specs, out_specs=out_specs, check_vma=False)
```

```python
import functools
import math

import jax
import jax.numpy as jnp
import numpy as np
from jax import lax
from jax.experimental import pallas as pl
from jax.experimental.pallas import tpu as pltpu
from jax.sharding import PartitionSpec as P

EPSILON = 1e-06
MESH = pl.DeviceIdType.MESH
BF = jnp.bfloat16
F32 = jnp.float32
HIDDEN_CHUNKS = (768, 768, 768)
RING = 4
ORDER = (
    ("product", 0, 1),
    ("s1", 0, 1),
    ("ordered", 0, 0),
    ("product", 0, 0),
    ("s1", 0, 0),
    ("more_loads", 0, 0),
    ("product", 1, 1),
    ("s2", 0, 1),
    ("s1", 1, 1),
    ("s2", 0, 0),
    ("product", 1, 0),
    ("s1", 1, 0),
    ("product", 3, 1),
    ("s3", 0, 0),
    ("product", 2, 0),
    ("product", 2, 1),
    ("s2", 1, 0),
    ("s2", 1, 1),
    ("s3", 0, 1),
    ("product", 3, 0),
    ("s1", 2, 1),
    ("final_order", 0, 0),
    ("s1", 2, 0),
    ("s3", 1, 0),
    ("s4", 0, 1),
    ("s3", 1, 1),
    ("s4", 0, 0),
    ("s1", 3, 1),
    ("s1", 3, 0),
    ("query_out", 0, 0),
    ("turns", 0, 0),
    ("s4", 1, 0),
    ("s4", 1, 1),
    ("attention", 0, 0),
    ("s2", 2, 0),
    ("s2", 2, 1),
    ("s2", 3, 1),
    ("hidden", 1, 0),
    ("s2", 3, 0),
    ("g1", 1, 0),
    ("hidden", 1, 1),
    ("attention", 1, 0),
    ("s3", 2, 1),
    ("attended", 0, 0),
    ("g1", 0, 1),
    ("g1", 0, 0),
    ("s3", 2, 0),
    ("s3", 3, 0),
    ("s4", 2, 0),
    ("s3", 3, 1),
    ("g1", 1, 1),
    ("g2", 0, 1),
    ("s4", 2, 1),
    ("s4", 3, 1),
    ("s4", 3, 0),
    ("g2", 0, 0),
    ("g2", 1, 0),
    ("hidden", 2, 0),
    ("g2", 1, 1),
    ("hidden", 2, 1),
    ("g1", 2, 1),
    ("g1", 2, 0),
    ("hidden", 3, 1),
    ("g1", 3, 1),
    ("g3", 0, 1),
    ("g3", 1, 0),
    ("hidden", 3, 0),
    ("g3", 0, 0),
    ("g2", 3, 1),
    ("g1", 3, 0),
    ("g3", 1, 1),
    ("g2", 2, 0),
    ("g2", 3, 0),
    ("g4", 1, 0),
    ("g4", 0, 1),
    ("g2", 2, 1),
    ("g4", 0, 0),
    ("g3", 2, 0),
    ("g3", 3, 1),
    ("second", 0, 1),
    ("g3", 2, 1),
    ("g4", 1, 1),
    ("g3", 3, 0),
    ("g4", 2, 0),
    ("second", 1, 0),
    ("second", 0, 0),
    ("g4", 2, 1),
    ("second", 1, 1),
    ("g4", 3, 0),
    ("g4", 3, 1),
    ("second", 2, 0),
    ("second", 2, 1),
    ("second_early", 3, 1),
    ("second_early", 3, 0),
    ("second_late", 3, 0),
    ("second_late", 3, 1),
)
SENDS, RECVS, LOADS = 39, 79, 19


def dot(a, b):
    return jnp.dot(a, b, preferred_element_type=F32)


def dot_t(a, b):
    return lax.dot_general(a, b, (((1,), (1,)), ((), ())), preferred_element_type=F32)


def iota(shape, dim):
    return lax.broadcasted_iota(jnp.int32, shape, dim)


def one_hot(mask):
    return jnp.where(mask, 1.0, 0.0).astype(BF)


def add_f32(*terms):
    total = terms[0].astype(F32)
    for term in terms[1:]:
        total = total + term.astype(F32)
    return total


class Scratch:
    def __init__(self):
        self.names, self.shapes = [], []

    def add(self, name, shape, dtype=BF):
        self.names.append(name)
        self.shapes.append(pltpu.VMEM(shape, dtype))


def query_width(f):
    return 768 + 128 * f


def scratch_plan(columns):
    s = Scratch()
    for f in range(2):
        for k in range(1 + len(HIDDEN_CHUNKS)):
            hc = 768 if k == 0 else HIDDEN_CHUNKS[k - 1]
            w = query_width(f) if k == 0 else 2 * hc
            t = (k, f)
            s.add(("w1",) + t, (columns, w))
            s.add(("part",) + t, (4, 4, 32, w))
            s.add(("r1",) + t, (2, 2, 32, w))
            s.add(("r2",) + t, (2, 4, 32, w))
            s.add(("q1",) + t, (2, 16, w))
            s.add(("q2",) + t, (2, 32, w))
            s.add(("ag",) + t, (4, 4, 32, hc))
            s.add(("w2",) + t, (hc, columns))
    s.add("keys", (2, 2048, 256))
    s.add("values", (2, 2048, 256))
    s.add("tk", (8, 64, columns))
    s.add("order", (2, 512, 512))
    s.add("xs", (2, 512, columns))
    s.add("acc", (16, 32, columns), F32)
    s.add("ob", (2, 4, 64, columns))
    s.add("fr", (4, 64, columns))
    s.add("fz1", (2, 32, columns))
    s.add("fz2", (2, 64, columns))
    s.add("qsend", (8, 32, 256))
    s.add("qrecv", (8, 32, 256))
    s.add("asend", (8, 32, 256))
    s.add("arecv", (8, 32, 256))
    s.add("inv", (32, 128), F32)
    s.add("turn", (2, 8, 128), F32)
    return s


class Half:
    pass


def kernel(
    plan_names,
    model_width,
    tok,
    gain,
    wq,
    wsh,
    wg,
    wu,
    wo,
    wd,
    kc,
    vc,
    lens,
    frequency,
    out,
    entries,
    *scratch,
):
    n = len(plan_names)
    b = dict(zip(plan_names, scratch[:n]))
    send_sem, recv_sem, local_sem = scratch[n:]
    columns = tok.shape[1]
    g = lax.axis_index("gx")
    q = lax.axis_index("yz")
    z, c = g // 2, lax.rem(g, 2)
    y, x = q // 4, lax.rem(q, 4)

    def step(v, d):
        return lax.rem(v + d + RING, RING)

    def at_x(d):
        return (g, y * 4 + step(x, d))

    def at_y(d):
        return (g, step(y, d) * 4 + x)

    def at_z(d):
        return (step(z, d) * 2 + c, q)

    partner = (z * 2 + 1 - c, q)

    sends, counts = [], {"send": 0, "recv": 0, "load": 0}

    def fresh(kind):
        counts[kind] += 1
        return counts[kind] - 1

    class Flight:
        def __init__(self, arriving):
            self.arriving, self.at = arriving, fresh("recv")

        def wait(self):
            pltpu.make_async_copy(self.arriving, self.arriving, recv_sem.at[self.at]).wait()

    def leaving(ref):
        at = fresh("send")
        sends.append((ref, at))
        return at

    def rc(src, dst, dev, flight, at):
        pltpu.make_async_remote_copy(
            src_ref=src,
            dst_ref=dst,
            send_sem=send_sem.at[at],
            recv_sem=recv_sem.at[flight.at],
            device_id=dev,
            device_id_type=MESH,
        ).start()

    loads = {}

    def load(name, whole, *pairs):
        at = fresh("load")
        for src, dst in pairs:
            pltpu.make_async_copy(src, dst, local_sem.at[at]).start()
        loads[name] = (whole, at)

    def loaded(name):
        whole, at = loads[name]
        pltpu.make_async_copy(whole, whole, local_sem.at[at]).wait()

    load("tok", b["tk"].at[g], (tok, b["tk"].at[g]))
    shared_at = pl.multiple_of(z * 128, 128)
    w1 = b["w1", 0, 1]
    load(
        ("w1", 0, 1),
        w1,
        (wq.at[:, 768:1536], w1.at[:, 0:768]),
        (wsh.at[:, pl.ds(shared_at, 128)], w1.at[:, 768:896]),
    )
    load(("w1", 0, 0), b["w1", 0, 0], (wq.at[:, 0:768], b["w1", 0, 0]))
    hidden_at = {}
    base = 0
    for k, hc in enumerate(HIDDEN_CHUNKS, 1):
        for f in range(2):
            hidden_at[k, f] = base
            base += hc

    def load_w1(k):
        hc = HIDDEN_CHUNKS[k - 1]
        for f in range(2):
            at = hidden_at[k, f]
            w1 = b["w1", k, f]
            load(
                ("w1", k, f),
                w1,
                (wg.at[:, at : at + hc], w1.at[:, 0:hc]),
                (wu.at[:, at : at + hc], w1.at[:, hc : 2 * hc]),
            )

    barrier = pltpu.get_barrier_semaphore()
    others = [lax.rem(g + d, 8) for d in range(1, 8)]
    peers = [at_x(1), at_x(-1), at_y(1), at_y(-1)] + [(o, q) for o in others]
    for peer in peers:
        pl.semaphore_signal(barrier, inc=1, device_id=peer, device_id_type=MESH)
    loaded("tok")
    pl.semaphore_wait(barrier, len(peers))

    tk = b["tk"]

    def block(zz):
        return zz * 2 + c

    zr, zl, zo = step(z, 1), step(z, -1), step(z, 2)
    parts = (pl.ds(0, 32), pl.ds(32, 32))

    token_sends = leaving(tk.at[0:7])
    crossing = Flight(tk.at[0:4])

    def send(blk, i, dev, flight=None):
        ref = tk.at[blk, parts[i]]
        flight = flight or Flight(ref)
        rc(ref, ref, dev, flight, token_sends)
        return flight

    def cross(blk, i):
        send(blk, i, partner, crossing)

    right_first = send(g, 0, at_z(1))
    left_first = send(g, 1, at_z(-1))
    right_last = send(g, 1, at_z(1))
    left_last = send(g, 0, at_z(-1))
    cross(g, 0)
    cross(g, 1)
    for k in range(1, 1 + len(HIDDEN_CHUNKS)):
        load_w1(k)
    row_i, col_i = iota((512, 512), 0), iota((512, 512), 1)
    tail = (((row_i >> 2) & 7) << 6) | (((row_i >> 1) & 1) << 5) | (row_i & 1)
    d1, d2 = (row_i >> 7) & 3, (row_i >> 5) & 3
    source = {0: tail | (d2 << 3) | (d1 << 1), 1: tail | (d1 << 3) | (d2 << 1)}
    order = b["order"]
    order[1] = one_hot(source[1] == col_i)
    right_first.wait()
    forward_r = send(block(zl), 0, at_z(1))
    cross(block(zl), 0)
    left_first.wait()
    forward_l = send(block(zr), 1, at_z(-1))
    cross(block(zr), 1)
    order[0] = one_hot(source[0] == col_i)
    right_last.wait()
    cross(block(zl), 1)
    left_last.wait()
    cross(block(zr), 0)
    forward_r.wait()
    cross(block(zo), 0)
    forward_l.wait()
    cross(block(zo), 1)
    crossing.wait()

    squares = []
    gain_row = gain[...].reshape(1, columns)

    def ordered(f):
        rows = dot(order[f], tk[...].reshape(512, columns))
        if f == 1:
            squares.append(jnp.sum(rows * rows, axis=1, keepdims=True))
        b["xs"][f] = (rows * gain_row).astype(BF)

    def more_loads():
        for k in range(1 + len(HIDDEN_CHUNKS)):
            for f in range(2):
                w2 = b["w2", k, f]
                if k == 0:
                    load(("w2", k, f), w2, (wo.at[768 * f : 768 * f + 768], w2))
                else:
                    at = hidden_at[k, f]
                    load(("w2", k, f), w2, (wd.at[at : at + HIDDEN_CHUNKS[k - 1]], w2))
        load("keys", b["keys"], (kc, b["keys"]))
        load("values", b["values"], (vc, b["values"]))

    lane = iota((1, 128), 1)
    mine = (lane >> 6) == c
    spread = 1.0 + (lane & 63).astype(F32) * (1.0 / 64.0)

    halves = {}
    for f in range(2):
        h = Half()
        first, second = (at_x, at_y) if f == 0 else (at_y, at_x)
        p1, p2 = (x, y) if f == 0 else (y, x)
        h.first, h.second, h.p1, h.p2 = first, second, p1, p2
        h.r1, h.l1, h.o1 = step(p1, 1), step(p1, -1), step(p1, 2)
        h.r2, h.l2, h.o2 = step(p2, 1), step(p2, -1), step(p2, 2)
        halves[f] = h
    cps = {}

    def product(k, f):
        loaded(("w1", k, f))
        part, w1 = b["part", k, f], b["w1", k, f]
        w = 768 if k == 0 else w1.shape[1]

        @pl.loop(0, w // 256)
        def _(i):
            at = pl.ds(pl.multiple_of(i * 256, 256), 256)
            value = dot(b["xs"][f], w1[:, at]).astype(BF)
            part[:, :, :, at] = value.reshape(4, 4, 32, 256)

        if k == 0 and f == 1:
            value = dot(b["xs"][f], w1[:, 768:896])
            value = jnp.where(mine, value, squares[0] * spread).astype(BF)
            part[:, :, :, 768:896] = value.reshape(4, 4, 32, 128)

    def s1(k, f):
        h, part, r1, r2 = halves[f], b["part", k, f], b["r1", k, f], b["r2", k, f]
        one, two, at = Flight(r1), Flight(r2), leaving(part.at[0:3])
        rc(part.at[h.o1, 0:2], r1.at[0], h.first(1), one, at)
        rc(part.at[h.o1, 2:4], r1.at[1], h.first(-1), one, at)
        rc(part.at[h.r1, 2:4], r2.at[0, 2:4], h.first(1), two, at)
        rc(part.at[h.l1, 0:2], r2.at[1, 0:2], h.first(-1), two, at)
        cps[k, f] = one, two, at

    def s2(k, f):
        h, part, r1, r2 = halves[f], b["part", k, f], b["r1", k, f], b["r2", k, f]
        one, two, at = cps[k, f]
        one.wait()
        part[h.r1, 0:2] = add_f32(part[h.r1, 0:2], r1[0]).astype(BF)
        rc(part.at[h.r1, 0:2], r2.at[0, 0:2], h.first(1), two, at)
        part[h.l1, 2:4] = add_f32(part[h.l1, 2:4], r1[1]).astype(BF)
        rc(part.at[h.l1, 2:4], r2.at[1, 2:4], h.first(-1), two, at)

    def s3(k, f):
        h, part, r2 = halves[f], b["part", k, f], b["r2", k, f]
        q1, q2 = b["q1", k, f], b["q2", k, f]
        cps[k, f][1].wait()

        def total(d):
            part[h.p1, d] = add_f32(part[h.p1, d], r2[0, d], r2[1, d]).astype(BF)

        one, two, at = Flight(q1), Flight(q2), leaving(part.at[0, 0:3])
        total(h.o2)
        rc(part.at[h.p1, h.o2, 0:16], q1.at[0], h.second(1), one, at)
        rc(part.at[h.p1, h.o2, 16:32], q1.at[1], h.second(-1), one, at)
        total(h.r2)
        rc(part.at[h.p1, h.r2, 16:32], q2.at[0, 16:32], h.second(1), two, at)
        total(h.l2)
        rc(part.at[h.p1, h.l2, 0:16], q2.at[1, 0:16], h.second(-1), two, at)
        total(h.p2)
        cps[k, f] = one, two, at

    def s4(k, f):
        h, part = halves[f], b["part", k, f]
        q1, q2 = b["q1", k, f], b["q2", k, f]
        one, two, at = cps[k, f]
        one.wait()
        part[h.p1, h.r2, 0:16] = add_f32(part[h.p1, h.r2, 0:16], q1[0]).astype(BF)
        rc(part.at[h.p1, h.r2, 0:16], q2.at[0, 0:16], h.second(1), two, at)
        part[h.p1, h.l2, 16:32] = add_f32(part[h.p1, h.l2, 16:32], q1[1]).astype(BF)
        rc(part.at[h.p1, h.l2, 16:32], q2.at[1, 16:32], h.second(-1), two, at)

    def s5(k, f, lo, hi):
        h, part, q2 = halves[f], b["part", k, f], b["q2", k, f]
        return add_f32(part[h.p1, h.p2, :, lo:hi], q2[0, :, lo:hi], q2[1, :, lo:hi])

    def s5_wait(k, f):
        cps[k, f][1].wait()

    def hidden(k, f):
        s5_wait(k, f)
        h, hc = halves[f], HIDDEN_CHUNKS[k - 1]
        inv = b["inv"][:, 0:1]
        gate = s5(k, f, 0, hc) * inv
        up = s5(k, f, hc, 2 * hc) * inv
        value = gate * (1.0 / (1.0 + jnp.exp(-gate))) * up
        b["ag", k, f][h.p2, h.p1] = value.astype(BF)

    def g1(k, f):
        h, ag = halves[f], b["ag", k, f]
        one, two, at = Flight(ag.at[0, 0:2]), Flight(ag.at[0, 0]), leaving(ag.at[0, 0:3])
        blk = ag.at[h.p2, h.p1]
        rc(blk, blk, h.first(1), one, at)
        rc(blk, blk, h.first(-1), one, at)
        cps["g", k, f] = one, two, at

    def g2(k, f):
        h, ag = halves[f], b["ag", k, f]
        one, two, at = cps["g", k, f]
        one.wait()
        blk = ag.at[h.p2, h.l1, 0:16]
        rc(blk, blk, h.first(1), two, at)
        blk = ag.at[h.p2, h.r1, 16:32]
        rc(blk, blk, h.first(-1), two, at)

    def g3(k, f):
        h, ag = halves[f], b["ag", k, f]
        cps["g", k, f][1].wait()
        one, two, at = Flight(ag.at[0:2]), Flight(ag.at[0]), leaving(ag.at[0:3])
        blk = ag.at[h.p2]
        rc(blk, blk, h.second(1), one, at)
        rc(blk, blk, h.second(-1), one, at)
        cps["g", k, f] = one, two, at

    def g4(k, f):
        h, ag = halves[f], b["ag", k, f]
        one, two, at = cps["g", k, f]
        one.wait()
        blk = ag.at[h.l2, 0:2]
        rc(blk, blk, h.second(1), two, at)
        blk = ag.at[h.r2, 2:4]
        rc(blk, blk, h.second(-1), two, at)

    first_product = [True]

    def second(k, f):
        cps["g", k, f][1].wait()
        loaded(("w2", k, f))
        ag, w2, acc = b["ag", k, f], b["w2", k, f], b["acc"]
        start = first_product[0]
        first_product[0] = False
        for lo, hi in ((0, 256), (256, 512), (512, columns)):
            value = dot(ag[...].reshape(512, ag.shape[3]), w2[:, lo:hi])
            value = value.reshape(16, 32, hi - lo)
            for i in range(16):
                to = i if f == 0 else i % 4 * 4 + i // 4
                if start:
                    acc[to, :, lo:hi] = value[i]
                else:
                    acc[to, :, lo:hi] += value[i]

    def second_rows(k, f, d):
        ag, w2, acc = b["ag", k, f], b["w2", k, f], b["acc"]
        value = dot(ag[d].reshape(128, ag.shape[3]), w2[...]).reshape(4, 32, columns)
        for i in range(4):
            at = d * 4 + i if f == 0 else i * 4 + d
            acc[at] += value[i]

    def second_early(k, f):
        h = halves[f]
        loaded(("w2", k, f))
        for d in (h.p2, h.l2, h.r2):
            second_rows(k, f, d)

    def second_late(k, f):
        cps["g", k, f][1].wait()
        second_rows(k, f, halves[f].o2)

    def exchange(send, recv):
        flight, at = Flight(recv.at[0:7]), leaving(send.at[0:7])
        for o in others:
            rc(send.at[o], recv.at[g], (o, q), flight, at)
        recv[g] = send[g]
        return flight

    def spread_rows(head):
        row, col = iota((256, 32), 0), iota((256, 32), 1)
        return one_hot((col == (((row >> 5) << 2) | (row & 3))) & (((row >> 2) & 7) == head))

    def collect_rows(head):
        row, col = iota((32, 256), 0), iota((32, 256), 1)
        return one_hot((row == (((col >> 5) << 2) | (col & 3))) & (((col >> 2) & 7) == head))

    def query_out():
        s5_wait(0, 0)
        s5_wait(0, 1)
        shared = s5(0, 1, 768, 896)
        total = jnp.sum(jnp.where(mine, 0.0, shared), axis=1, keepdims=True) * (1.0 / 95.5)
        inv = lax.rsqrt(total / model_width + EPSILON)
        b["inv"][...] = jnp.broadcast_to(inv, (32, 128))
        shared = jnp.where(mine, shared * inv, 0.0)
        low = lax.rem(z, 2) == 0
        shared = jnp.concatenate([jnp.where(low, shared, 0.0), jnp.where(low, 0.0, shared)], axis=1)
        rows = dot(spread_rows(6), shared.astype(BF))
        for f in range(2):
            for i in range(3):
                piece = (s5(0, f, i * 256, i * 256 + 256) * inv).astype(BF)
                rows = rows + dot(spread_rows(f * 3 + i), piece)
        b["qsend"][...] = rows.astype(BF).reshape(8, 32, 256)
        cps["q"] = exchange(b["qsend"], b["qrecv"])

    def rotate(rows):
        count = rows.shape[0]
        rows = rows.reshape(count // 8, 8, 256)
        front, back = rows[:, :, :128], rows[:, :, 128:]
        cosine, sine = b["turn"][0][None], b["turn"][1][None]
        return jnp.concatenate(
            [front * cosine - back * sine, back * cosine + front * sine], axis=2
        ).reshape(count, 256)

    def turns():
        row = iota((8, 128), 0)
        position = jnp.where((row & 1) == 0, lens[0], lens[1]) + ((row >> 1) & 1)
        angles = position.astype(F32) * frequency[...]
        b["turn"][0] = jnp.cos(angles)
        b["turn"][1] = jnp.sin(angles)

    def attention():
        cps["q"].wait()
        loaded("keys")
        loaded("values")
        raw = b["qrecv"][...].reshape(256, 256)
        queries = rotate(raw.astype(F32)).astype(BF)
        row, col = iota((128, 256), 0), iota((128, 256), 1)
        pick = (row < 4) & ((col & 31) == row + 24)
        key_now = rotate(dot(one_hot(pick & (col < 128)), raw)).astype(BF)
        value_now = dot(one_hot(pick & (col >= 128)), raw).astype(BF)
        for i, part in enumerate((key_now, value_now)):
            fresh_rows = part[0:16].astype(F32)
            for t in range(2):
                entries[t, :, i * 256 : i * 256 + 256] = fresh_rows[2 * t : 2 * t + 2].astype(BF)
        cps["rows"] = queries, key_now, value_now
        attention_row(0)

    def attention_row(j):
        queries, key_now, value_now = cps["rows"]
        row, col = iota((128, 256), 0), iota((128, 256), 1)
        chosen = one_hot(col == (((row >> 4) << 5) + ((row & 15) << 1) + j))
        heads = dot(chosen, queries).astype(BF)
        scores = dot_t(heads, b["keys"][j]) * (1.0 / 16.0)
        live = iota(scores.shape, 1) < lens[j]
        scores = jnp.where(live, scores, -jnp.inf)
        now = dot_t(heads, key_now) * (1.0 / 16.0)
        r, n_ = iota((128, 128), 0), iota((128, 128), 1)
        now = jnp.where((n_ < 4) & ((n_ & 1) == j) & ((n_ >> 1) <= (r & 1)), now, -jnp.inf)
        top = jnp.maximum(
            jnp.max(scores, axis=1, keepdims=True), jnp.max(now, axis=1, keepdims=True)
        )
        scores = jnp.exp(scores - top)
        now = jnp.exp(now - top)
        under = jnp.sum(scores, axis=1, keepdims=True) + jnp.sum(now, axis=1, keepdims=True)
        scale = 1.0 / under
        mixed = dot((scores * scale).astype(BF), b["values"][j]) + dot(
            (now * scale).astype(BF), value_now
        )
        brow, bcol = iota((256, 128), 0), iota((256, 128), 1)
        back = one_hot(brow == (((bcol >> 4) << 5) + ((bcol & 15) << 1) + j))
        term = dot(back, mixed.astype(BF))
        if j == 0:
            cps["term"] = term
            return
        result = cps["term"] + term
        b["asend"][...] = result.astype(BF).reshape(8, 32, 256)
        cps["a"] = exchange(b["asend"], b["arecv"])

    def attended():
        cps["a"].wait()
        raw = b["arecv"][...].reshape(256, 256)
        for f in range(2):
            h = halves[f]
            for i in range(3):
                value = dot(collect_rows(f * 3 + i), raw).astype(BF)
                b["ag", 0, f][h.p2, h.p1, :, i * 256 : i * 256 + 256] = value

    def final_order():
        gx_o = (((row_i >> 6) & 3) << 1) | (row_i >> 8)
        wanted = (((row_i >> 1) & 15) << 5) | (gx_o << 2) | (((row_i >> 5) & 1) << 1) | (row_i & 1)
        order[0] = one_hot(wanted == col_i)

    stages = {
        "ordered": lambda k, f: ordered(f),
        "query_out": lambda k, f: query_out(),
        "attention": lambda k, f: attention_row(1) if k else attention(),
        "attended": lambda k, f: attended(),
        "turns": lambda k, f: turns(),
        "final_order": lambda k, f: final_order(),
        "more_loads": lambda k, f: more_loads(),
    }
    for stage in (product, s1, s2, s3, s4, hidden, g1, g2, g3, g4, second, second_early, second_late):
        stages[stage.__name__] = stage

    ordered(1)
    for name, k, f in ORDER:
        stages[name](k, f)

    ob, fr, fz1, fz2 = b["ob"], b["fr"], b["fz1"], b["fz2"]
    spans = (slice(0, 384), slice(384, columns))
    top, low = slice(0, 32), slice(32, 64)
    crossed = []
    for span in spans:
        rows = b["acc"][:, :, span].reshape(512, -1).astype(BF)
        ob[:, :, :, span] = dot(order[0], rows).astype(BF).reshape(2, 4, 64, -1)
        flight = Flight(fr.at[:, :, span])
        rc(ob.at[1 - c, :, :, span], fr.at[:, :, span], partner, flight, leaving(fr.at[:, :, span]))
        crossed.append(flight)
    waves = []
    for i, span in enumerate(spans):
        crossed[i].wait()

        def add_partner(zz):
            ob[c, zz, :, span] = add_f32(ob[c, zz, :, span], fr[zz, :, span]).astype(BF)

        one, two = Flight(fz1.at[:, :, span]), Flight(fz2.at[:, :, span])
        at = leaving(fr.at[0:3, :, span])
        add_partner(zo)
        rc(ob.at[c, zo, top, span], fz1.at[0, :, span], at_z(1), one, at)
        rc(ob.at[c, zo, low, span], fz1.at[1, :, span], at_z(-1), one, at)
        add_partner(zr)
        rc(ob.at[c, zr, low, span], fz2.at[0, low, span], at_z(1), two, at)
        add_partner(zl)
        rc(ob.at[c, zl, top, span], fz2.at[1, top, span], at_z(-1), two, at)
        waves.append((one, two, at))
    for i, span in enumerate(spans):
        one, two, at = waves[i]
        one.wait()
        ob[c, zr, top, span] = add_f32(ob[c, zr, top, span], fz1[0, :, span]).astype(BF)
        rc(ob.at[c, zr, top, span], fz2.at[0, top, span], at_z(1), two, at)
        ob[c, zl, low, span] = add_f32(ob[c, zl, low, span], fz1[1, :, span]).astype(BF)
        rc(ob.at[c, zl, low, span], fz2.at[1, low, span], at_z(-1), two, at)
    for i, span in enumerate(spans):
        own = add_f32(ob[c, z, :, span], fr[z, :, span])
        waves[i][1].wait()
        own = own + fz2[0, :, span].astype(F32) + fz2[1, :, span].astype(F32)
        out[:, :, span] = own.reshape(2, 32, -1)
    for ref, at in sends:
        pltpu.make_async_copy(ref, ref, send_sem.at[at]).wait()
    assert counts == {"send": SENDS, "recv": RECVS, "load": LOADS}, counts


def local(
    tokens,
    norm_gain,
    w_query,
    w_shared,
    w_gate,
    w_up,
    w_out,
    w_down,
    key_cache,
    value_cache,
    lengths,
):
    steps, block_rows, columns = tokens.shape
    model_width = columns * lax.axis_size("yz")
    frequency = np.exp(np.arange(128, dtype=np.float32) * np.float32(-2.0 * math.log(10000.0) / 256))
    plan = scratch_plan(columns)
    hbm = pl.BlockSpec(memory_space=pl.ANY)
    vmem = pl.BlockSpec(memory_space=pltpu.VMEM)
    smem = pl.BlockSpec(memory_space=pltpu.SMEM)
    layer, entries = pl.pallas_call(
        functools.partial(kernel, plan.names, model_width),
        out_shape=(
            jax.ShapeDtypeStruct((steps, block_rows, columns), F32),
            jax.ShapeDtypeStruct((2, 2, 512), BF),
        ),
        in_specs=[hbm, vmem] + [hbm] * 8 + [smem, vmem],
        out_specs=(vmem, vmem),
        scratch_shapes=plan.shapes
        + [
            pltpu.SemaphoreType.DMA((SENDS,)),
            pltpu.SemaphoreType.DMA((RECVS,)),
            pltpu.SemaphoreType.DMA((LOADS,)),
        ],
        compiler_params=pltpu.CompilerParams(
            collective_id=0, has_side_effects=True, vmem_limit_bytes=64 << 20
        ),
        cost_estimate=pl.CostEstimate(
            flops=12 * 10**9, bytes_accessed=28 * 10**6, transcendentals=10**6
        ),
    )(
        tokens.reshape(steps * block_rows, columns),
        norm_gain,
        w_query,
        w_shared,
        w_gate,
        w_up,
        w_out,
        w_down,
        key_cache,
        value_cache,
        lengths,
        jnp.asarray(frequency[None]),
    )
    return (tokens.astype(F32) + layer).astype(BF), entries


def solution(mesh):
    in_specs = (
        P(None, "gx", "yz"),
        P("yz"),
        P("yz", "gx"),
        P("yz", None),
        P("yz", "gx"),
        P("yz", "gx"),
        P("gx", "yz"),
        P("gx", "yz"),
        P(("gx", "yz"), None, None),
        P(("gx", "yz"), None, None),
        P(("gx", "yz")),
    )
    out_specs = (P(None, "gx", "yz"), P(None, ("gx", "yz"), None))
    return jax.shard_map(local, mesh=mesh, in_specs=in_specs, out_specs=out_specs, check_vma=False)
```

```python
import functools
import math

import jax
import jax.numpy as jnp
import numpy as np
from jax import lax
from jax.experimental import pallas as pl
from jax.experimental.pallas import tpu as pltpu
from jax.sharding import PartitionSpec as P

EPSILON = 1e-06
MESH = pl.DeviceIdType.MESH
BF = jnp.bfloat16
F32 = jnp.float32
HIDDEN_CHUNKS = (768, 768, 768)
RING = 4
ORDER = (
    ("more_loads", 0, 0),
    ("product", 1, 1),
    ("s2", 0, 1),
    ("s1", 1, 1),
    ("s2", 0, 0),
    ("product", 1, 0),
    ("s1", 1, 0),
    ("product", 3, 1),
    ("s3", 0, 0),
    ("product", 2, 0),
    ("product", 2, 1),
    ("s2", 1, 0),
    ("s2", 1, 1),
    ("s3", 0, 1),
    ("product", 3, 0),
    ("s1", 2, 1),
    ("final_order", 0, 0),
    ("s1", 2, 0),
    ("s3", 1, 0),
    ("s4", 0, 1),
    ("s3", 1, 1),
    ("s4", 0, 0),
    ("s1", 3, 1),
    ("s1", 3, 0),
    ("query_out", 0, 0),
    ("turns", 0, 0),
    ("s4", 1, 0),
    ("s4", 1, 1),
    ("attention", 0, 0),
    ("s2", 2, 0),
    ("s2", 2, 1),
    ("s2", 3, 1),
    ("hidden", 1, 0),
    ("s2", 3, 0),
    ("g1", 1, 0),
    ("hidden", 1, 1),
    ("attention", 1, 0),
    ("s3", 2, 1),
    ("attended", 0, 0),
    ("g1", 0, 1),
    ("g1", 0, 0),
    ("s3", 2, 0),
    ("s3", 3, 0),
    ("s4", 2, 0),
    ("s3", 3, 1),
    ("g1", 1, 1),
    ("g2", 0, 1),
    ("s4", 2, 1),
    ("s4", 3, 1),
    ("s4", 3, 0),
    ("g2", 0, 0),
    ("g2", 1, 0),
    ("hidden", 2, 0),
    ("g2", 1, 1),
    ("hidden", 2, 1),
    ("g1", 2, 1),
    ("g1", 2, 0),
    ("hidden", 3, 1),
    ("g1", 3, 1),
    ("g3", 0, 1),
    ("g3", 1, 0),
    ("hidden", 3, 0),
    ("g3", 0, 0),
    ("g2", 3, 1),
    ("g1", 3, 0),
    ("g3", 1, 1),
    ("g2", 2, 0),
    ("g2", 3, 0),
    ("g4", 1, 0),
    ("g4", 0, 1),
    ("g2", 2, 1),
    ("g4", 0, 0),
    ("g3", 2, 0),
    ("g3", 3, 1),
    ("second", 0, 1),
    ("g3", 2, 1),
    ("g4", 1, 1),
    ("g3", 3, 0),
    ("g4", 2, 0),
    ("second", 1, 0),
    ("second", 0, 0),
    ("g4", 2, 1),
    ("second", 1, 1),
    ("g4", 3, 0),
    ("g4", 3, 1),
    ("second", 2, 0),
    ("second", 2, 1),
    ("second_early", 3, 1),
    ("second_early", 3, 0),
    ("second_late", 3, 0),
    ("second_late", 3, 1),
)
SENDS, RECVS, LOADS = 39, 80, 19


def dot(a, b):
    return jnp.dot(a, b, preferred_element_type=F32)


def dot_t(a, b):
    return lax.dot_general(a, b, (((1,), (1,)), ((), ())), preferred_element_type=F32)


def iota(shape, dim):
    return lax.broadcasted_iota(jnp.int32, shape, dim)


def one_hot(mask):
    return jnp.where(mask, 1.0, 0.0).astype(BF)


def add_f32(*terms):
    total = terms[0].astype(F32)
    for term in terms[1:]:
        total = total + term.astype(F32)
    return total


class Scratch:
    def __init__(self):
        self.names, self.shapes = [], []

    def add(self, name, shape, dtype=BF):
        self.names.append(name)
        self.shapes.append(pltpu.VMEM(shape, dtype))


def query_width(f):
    return 768 + 128 * f


def scratch_plan(columns):
    s = Scratch()
    for f in range(2):
        for k in range(1 + len(HIDDEN_CHUNKS)):
            hc = 768 if k == 0 else HIDDEN_CHUNKS[k - 1]
            w = query_width(f) if k == 0 else 2 * hc
            t = (k, f)
            s.add(("w1",) + t, (columns, w))
            s.add(("part",) + t, (4, 4, 32, w))
            s.add(("r1",) + t, (2, 2, 32, w))
            s.add(("r2",) + t, (2, 4, 32, w))
            s.add(("q1",) + t, (2, 16, w))
            s.add(("q2",) + t, (2, 32, w))
            s.add(("ag",) + t, (4, 4, 32, hc))
            s.add(("w2",) + t, (hc, columns))
    s.add("keys", (2, 2048, 256))
    s.add("values", (2, 2048, 256))
    s.add("tk", (8, 64, columns))
    s.add("order", (2, 512, 512))
    s.add("xs", (2, 2, 256, columns))
    s.add("acc", (16, 32, columns), F32)
    s.add("ob", (2, 4, 64, columns))
    s.add("fr", (4, 64, columns))
    s.add("fz1", (2, 32, columns))
    s.add("fz2", (2, 64, columns))
    s.add("qsend", (8, 32, 256))
    s.add("qrecv", (8, 32, 256))
    s.add("asend", (8, 32, 256))
    s.add("arecv", (8, 32, 256))
    s.add("inv", (32, 128), F32)
    s.add("turn", (2, 8, 128), F32)
    return s


class Half:
    pass


def kernel(
    plan_names,
    model_width,
    tok,
    gain,
    wq,
    wsh,
    wg,
    wu,
    wo,
    wd,
    kc,
    vc,
    lens,
    frequency,
    out,
    entries,
    *scratch,
):
    n = len(plan_names)
    b = dict(zip(plan_names, scratch[:n]))
    send_sem, recv_sem, local_sem = scratch[n:]
    columns = tok.shape[1]
    g = lax.axis_index("gx")
    q = lax.axis_index("yz")
    z, c = g // 2, lax.rem(g, 2)
    y, x = q // 4, lax.rem(q, 4)

    def step(v, d):
        return lax.rem(v + d + RING, RING)

    def at_x(d):
        return (g, y * 4 + step(x, d))

    def at_y(d):
        return (g, step(y, d) * 4 + x)

    def at_z(d):
        return (step(z, d) * 2 + c, q)

    partner = (z * 2 + 1 - c, q)

    sends, counts = [], {"send": 0, "recv": 0, "load": 0}

    def fresh(kind):
        counts[kind] += 1
        return counts[kind] - 1

    class Flight:
        def __init__(self, arriving):
            self.arriving, self.at = arriving, fresh("recv")

        def wait(self):
            pltpu.make_async_copy(self.arriving, self.arriving, recv_sem.at[self.at]).wait()

    def leaving(ref):
        at = fresh("send")
        sends.append((ref, at))
        return at

    def rc(src, dst, dev, flight, at):
        pltpu.make_async_remote_copy(
            src_ref=src,
            dst_ref=dst,
            send_sem=send_sem.at[at],
            recv_sem=recv_sem.at[flight.at],
            device_id=dev,
            device_id_type=MESH,
        ).start()

    loads = {}

    def load(name, whole, *pairs):
        at = fresh("load")
        for src, dst in pairs:
            pltpu.make_async_copy(src, dst, local_sem.at[at]).start()
        loads[name] = (whole, at)

    def loaded(name):
        whole, at = loads[name]
        pltpu.make_async_copy(whole, whole, local_sem.at[at]).wait()

    barrier = pltpu.get_barrier_semaphore()
    others = [lax.rem(g + d, 8) for d in range(1, 8)]
    peers = [at_x(1), at_x(-1), at_y(1), at_y(-1)] + [(o, q) for o in others]
    for peer in peers:
        pl.semaphore_signal(barrier, inc=1, device_id=peer, device_id_type=MESH)

    load("tok", b["tk"].at[g], (tok, b["tk"].at[g]))
    shared_at = pl.multiple_of(z * 128, 128)
    w1 = b["w1", 0, 1]
    load(
        ("w1", 0, 1),
        w1,
        (wq.at[:, 768:1536], w1.at[:, 0:768]),
        (wsh.at[:, pl.ds(shared_at, 128)], w1.at[:, 768:896]),
    )
    load(("w1", 0, 0), b["w1", 0, 0], (wq.at[:, 0:768], b["w1", 0, 0]))
    hidden_at = {}
    base = 0
    for k, hc in enumerate(HIDDEN_CHUNKS, 1):
        for f in range(2):
            hidden_at[k, f] = base
            base += hc

    def load_w1(k):
        hc = HIDDEN_CHUNKS[k - 1]
        for f in range(2):
            at = hidden_at[k, f]
            w1 = b["w1", k, f]
            load(
                ("w1", k, f),
                w1,
                (wg.at[:, at : at + hc], w1.at[:, 0:hc]),
                (wu.at[:, at : at + hc], w1.at[:, hc : 2 * hc]),
            )

    loaded("tok")
    pl.semaphore_wait(barrier, len(peers))

    tk = b["tk"]

    def block(zz):
        return zz * 2 + c

    zr, zl, zo = step(z, 1), step(z, -1), step(z, 2)
    parts = (pl.ds(0, 32), pl.ds(32, 32))

    token_sends = leaving(tk.at[0:7])
    near, far = Flight(tk.at[0:2]), Flight(tk.at[0:2])

    def send(blk, i, dev, flight=None):
        ref = tk.at[blk, parts[i]]
        flight = flight or Flight(ref)
        rc(ref, ref, dev, flight, token_sends)
        return flight

    def cross(blk, i, flight):
        send(blk, i, partner, flight)

    left_first = send(g, 1, at_z(-1))
    right_first = send(g, 0, at_z(1))
    left_last = send(g, 0, at_z(-1))
    right_last = send(g, 1, at_z(1))
    cross(g, 0, near)
    cross(g, 1, near)
    for k in range(1, 1 + len(HIDDEN_CHUNKS)):
        load_w1(k)
    row_i, col_i = iota((256, 256), 0), iota((256, 256), 1)
    tail = (((row_i >> 2) & 3) << 6) | (((row_i >> 1) & 1) << 5) | (row_i & 1)
    d1, d2 = (row_i >> 6) & 3, (row_i >> 4) & 3
    order = b["order"]
    order[0, 0:256, 0:256] = one_hot((tail | (d2 << 3) | (d1 << 1)) == col_i)
    order[1, 0:256, 0:256] = one_hot((tail | (d1 << 3) | (d2 << 1)) == col_i)
    left_first.wait()
    forward_l = send(block(zr), 1, at_z(-1))
    cross(block(zr), 1, near)
    right_first.wait()
    forward_r = send(block(zl), 0, at_z(1))
    left_last.wait()
    cross(block(zr), 0, near)
    cross(block(zl), 0, far)
    right_last.wait()
    cross(block(zl), 1, far)
    near.wait()

    squares = {}
    gain_row = gain[...].reshape(1, columns)

    def position(gx):
        return ((((gx >> 1) + 4 - z) & 3) << 1) | (gx & 1)

    def ordered(f, group):
        planes = [tk[pl.ds(step(z, 2 * group + i) * 2, 2)].reshape(128, columns) for i in range(2)]
        rows = dot(order[f, 0:256, 0:256], jnp.concatenate(planes, axis=0))
        if f == 1:
            squares[group] = jnp.sum(rows * rows, axis=1, keepdims=True)
        b["xs"][f, group] = (rows * gain_row).astype(BF)

    def more_loads():
        for k in range(1 + len(HIDDEN_CHUNKS)):
            for f in range(2):
                w2 = b["w2", k, f]
                if k == 0:
                    load(("w2", k, f), w2, (wo.at[768 * f : 768 * f + 768], w2))
                else:
                    at = hidden_at[k, f]
                    load(("w2", k, f), w2, (wd.at[at : at + HIDDEN_CHUNKS[k - 1]], w2))
        load("keys", b["keys"], (kc, b["keys"]))
        load("values", b["values"], (vc, b["values"]))

    lane = iota((1, 128), 1)
    mine = (lane >> 6) == c
    spread = 1.0 + (lane & 63).astype(F32) * (1.0 / 64.0)

    halves = {}
    for f in range(2):
        h = Half()
        first, second = (at_x, at_y) if f == 0 else (at_y, at_x)
        p1, p2 = (x, y) if f == 0 else (y, x)
        h.first, h.second, h.p1, h.p2 = first, second, p1, p2
        h.r1, h.l1, h.o1 = step(p1, 1), step(p1, -1), step(p1, 2)
        h.r2, h.l2, h.o2 = step(p2, 1), step(p2, -1), step(p2, 2)
        halves[f] = h
    cps = {}

    def product(k, f):
        loaded(("w1", k, f))
        part, w1, xs = b["part", k, f], b["w1", k, f], b["xs"]

        @pl.loop(0, w1.shape[1] // 256)
        def _(i):
            at = pl.ds(pl.multiple_of(i * 256, 256), 256)
            value = dot(xs[f].reshape(512, columns), w1[:, at]).astype(BF)
            value = value.reshape(2, 4, 4, 16, 256)
            part[:, :, 0:16, at] = value[0]
            part[:, :, 16:32, at] = value[1]

    def product_group(f, group):
        if group == 0:
            loaded(("w1", 0, f))
        part, w1, xs = b["part", 0, f], b["w1", 0, f], b["xs"]
        lines = slice(16 * group, 16 * group + 16)
        for i in range(3):
            at = slice(i * 256, i * 256 + 256)
            value = dot(xs[f, group], w1[:, at]).astype(BF)
            part[:, :, lines, at] = value.reshape(4, 4, 16, 256)
        if f == 1:
            value = dot(xs[f, group], w1[:, 768:896])
            value = jnp.where(mine, value, squares[group] * spread).astype(BF)
            part[:, :, lines, 768:896] = value.reshape(4, 4, 16, 128)

    def s1_group(f, group):
        h, part, r1, r2 = halves[f], b["part", 0, f], b["r1", 0, f], b["r2", 0, f]
        if group == 0:
            cps[0, f] = Flight(r1), Flight(r2), leaving(part.at[0:3])
        one, two, at = cps[0, f]
        lines = slice(16 * group, 16 * group + 16)
        rc(part.at[h.o1, 0:2, lines], r1.at[0, :, lines], h.first(1), one, at)
        rc(part.at[h.o1, 2:4, lines], r1.at[1, :, lines], h.first(-1), one, at)
        rc(part.at[h.r1, 2:4, lines], r2.at[0, 2:4, lines], h.first(1), two, at)
        rc(part.at[h.l1, 0:2, lines], r2.at[1, 0:2, lines], h.first(-1), two, at)

    def s1(k, f):
        h, part, r1, r2 = halves[f], b["part", k, f], b["r1", k, f], b["r2", k, f]
        one, two, at = Flight(r1), Flight(r2), leaving(part.at[0:3])
        rc(part.at[h.o1, 0:2], r1.at[0], h.first(1), one, at)
        rc(part.at[h.o1, 2:4], r1.at[1], h.first(-1), one, at)
        rc(part.at[h.r1, 2:4], r2.at[0, 2:4], h.first(1), two, at)
        rc(part.at[h.l1, 0:2], r2.at[1, 0:2], h.first(-1), two, at)
        cps[k, f] = one, two, at

    def s2(k, f):
        h, part, r1, r2 = halves[f], b["part", k, f], b["r1", k, f], b["r2", k, f]
        one, two, at = cps[k, f]
        one.wait()
        part[h.r1, 0:2] = add_f32(part[h.r1, 0:2], r1[0]).astype(BF)
        rc(part.at[h.r1, 0:2], r2.at[0, 0:2], h.first(1), two, at)
        part[h.l1, 2:4] = add_f32(part[h.l1, 2:4], r1[1]).astype(BF)
        rc(part.at[h.l1, 2:4], r2.at[1, 2:4], h.first(-1), two, at)

    def s3(k, f):
        h, part, r2 = halves[f], b["part", k, f], b["r2", k, f]
        q1, q2 = b["q1", k, f], b["q2", k, f]
        cps[k, f][1].wait()

        def total(d):
            part[h.p1, d] = add_f32(part[h.p1, d], r2[0, d], r2[1, d]).astype(BF)

        one, two, at = Flight(q1), Flight(q2), leaving(part.at[0, 0:3])
        total(h.o2)
        rc(part.at[h.p1, h.o2, 0:16], q1.at[0], h.second(1), one, at)
        rc(part.at[h.p1, h.o2, 16:32], q1.at[1], h.second(-1), one, at)
        total(h.r2)
        rc(part.at[h.p1, h.r2, 16:32], q2.at[0, 16:32], h.second(1), two, at)
        total(h.l2)
        rc(part.at[h.p1, h.l2, 0:16], q2.at[1, 0:16], h.second(-1), two, at)
        total(h.p2)
        cps[k, f] = one, two, at

    def s4(k, f):
        h, part = halves[f], b["part", k, f]
        q1, q2 = b["q1", k, f], b["q2", k, f]
        one, two, at = cps[k, f]
        one.wait()
        part[h.p1, h.r2, 0:16] = add_f32(part[h.p1, h.r2, 0:16], q1[0]).astype(BF)
        rc(part.at[h.p1, h.r2, 0:16], q2.at[0, 0:16], h.second(1), two, at)
        part[h.p1, h.l2, 16:32] = add_f32(part[h.p1, h.l2, 16:32], q1[1]).astype(BF)
        rc(part.at[h.p1, h.l2, 16:32], q2.at[1, 16:32], h.second(-1), two, at)

    def s5(k, f, lo, hi):
        h, part, q2 = halves[f], b["part", k, f], b["q2", k, f]
        return add_f32(part[h.p1, h.p2, :, lo:hi], q2[0, :, lo:hi], q2[1, :, lo:hi])

    def s5_wait(k, f):
        cps[k, f][1].wait()

    def hidden(k, f):
        s5_wait(k, f)
        h, hc = halves[f], HIDDEN_CHUNKS[k - 1]
        inv = b["inv"][:, 0:1]
        gate = s5(k, f, 0, hc) * inv
        up = s5(k, f, hc, 2 * hc) * inv
        value = gate * (1.0 / (1.0 + jnp.exp(-gate))) * up
        b["ag", k, f][h.p2, h.p1] = value.astype(BF)

    def g1(k, f):
        h, ag = halves[f], b["ag", k, f]
        one, two, at = Flight(ag.at[0, 0:2]), Flight(ag.at[0, 0]), leaving(ag.at[0, 0:3])
        blk = ag.at[h.p2, h.p1]
        rc(blk, blk, h.first(1), one, at)
        rc(blk, blk, h.first(-1), one, at)
        cps["g", k, f] = one, two, at

    def g2(k, f):
        h, ag = halves[f], b["ag", k, f]
        one, two, at = cps["g", k, f]
        one.wait()
        blk = ag.at[h.p2, h.l1, 0:16]
        rc(blk, blk, h.first(1), two, at)
        blk = ag.at[h.p2, h.r1, 16:32]
        rc(blk, blk, h.first(-1), two, at)

    def g3(k, f):
        h, ag = halves[f], b["ag", k, f]
        cps["g", k, f][1].wait()
        one, two, at = Flight(ag.at[0:2]), Flight(ag.at[0]), leaving(ag.at[0:3])
        blk = ag.at[h.p2]
        rc(blk, blk, h.second(1), one, at)
        rc(blk, blk, h.second(-1), one, at)
        cps["g", k, f] = one, two, at

    def g4(k, f):
        h, ag = halves[f], b["ag", k, f]
        one, two, at = cps["g", k, f]
        one.wait()
        blk = ag.at[h.l2, 0:2]
        rc(blk, blk, h.second(1), two, at)
        blk = ag.at[h.r2, 2:4]
        rc(blk, blk, h.second(-1), two, at)

    first_product = [True]

    def second(k, f):
        cps["g", k, f][1].wait()
        loaded(("w2", k, f))
        ag, w2, acc = b["ag", k, f], b["w2", k, f], b["acc"]
        start = first_product[0]
        first_product[0] = False
        for lo, hi in ((0, 256), (256, 512), (512, columns)):
            value = dot(ag[...].reshape(512, ag.shape[3]), w2[:, lo:hi])
            value = value.reshape(16, 32, hi - lo)
            for i in range(16):
                to = i if f == 0 else i % 4 * 4 + i // 4
                if start:
                    acc[to, :, lo:hi] = value[i]
                else:
                    acc[to, :, lo:hi] += value[i]

    def second_rows(k, f, d):
        ag, w2, acc = b["ag", k, f], b["w2", k, f], b["acc"]
        value = dot(ag[d].reshape(128, ag.shape[3]), w2[...]).reshape(4, 32, columns)
        for i in range(4):
            at = d * 4 + i if f == 0 else i * 4 + d
            acc[at] += value[i]

    def second_early(k, f):
        h = halves[f]
        loaded(("w2", k, f))
        for d in (h.p2, h.l2, h.r2):
            second_rows(k, f, d)

    def second_late(k, f):
        cps["g", k, f][1].wait()
        second_rows(k, f, halves[f].o2)

    def exchange(send, recv):
        flight, at = Flight(recv.at[0:7]), leaving(send.at[0:7])
        for o in others:
            rc(send.at[o], recv.at[g], (o, q), flight, at)
        recv[g] = send[g]
        return flight

    def spread_rows(head):
        row, col = iota((256, 32), 0), iota((256, 32), 1)
        return one_hot((col == ((position(row >> 5) << 2) | (row & 3))) & (((row >> 2) & 7) == head))

    def collect_rows(head):
        row, col = iota((32, 256), 0), iota((32, 256), 1)
        return one_hot((row == ((position(col >> 5) << 2) | (col & 3))) & (((col >> 2) & 7) == head))

    def query_out():
        s5_wait(0, 0)
        s5_wait(0, 1)
        shared = s5(0, 1, 768, 896)
        total = jnp.sum(jnp.where(mine, 0.0, shared), axis=1, keepdims=True) * (1.0 / 95.5)
        inv = lax.rsqrt(total / model_width + EPSILON)
        b["inv"][...] = jnp.broadcast_to(inv, (32, 128))
        shared = jnp.where(mine, shared * inv, 0.0)
        low = lax.rem(z, 2) == 0
        shared = jnp.concatenate([jnp.where(low, shared, 0.0), jnp.where(low, 0.0, shared)], axis=1)
        rows = dot(spread_rows(6), shared.astype(BF))
        for f in range(2):
            for i in range(3):
                piece = (s5(0, f, i * 256, i * 256 + 256) * inv).astype(BF)
                rows = rows + dot(spread_rows(f * 3 + i), piece)
        b["qsend"][...] = rows.astype(BF).reshape(8, 32, 256)
        cps["q"] = exchange(b["qsend"], b["qrecv"])

    def rotate(rows):
        count = rows.shape[0]
        rows = rows.reshape(count // 8, 8, 256)
        front, back = rows[:, :, :128], rows[:, :, 128:]
        cosine, sine = b["turn"][0][None], b["turn"][1][None]
        return jnp.concatenate(
            [front * cosine - back * sine, back * cosine + front * sine], axis=2
        ).reshape(count, 256)

    def turns():
        row = iota((8, 128), 0)
        position = jnp.where((row & 1) == 0, lens[0], lens[1]) + ((row >> 1) & 1)
        angles = position.astype(F32) * frequency[...]
        b["turn"][0] = jnp.cos(angles)
        b["turn"][1] = jnp.sin(angles)

    def attention():
        cps["q"].wait()
        loaded("keys")
        loaded("values")
        raw = b["qrecv"][...].reshape(256, 256)
        queries = rotate(raw.astype(F32)).astype(BF)
        row, col = iota((128, 256), 0), iota((128, 256), 1)
        pick = (row < 4) & ((col & 31) == row + 24)
        key_now = rotate(dot(one_hot(pick & (col < 128)), raw)).astype(BF)
        value_now = dot(one_hot(pick & (col >= 128)), raw).astype(BF)
        for i, part in enumerate((key_now, value_now)):
            fresh_rows = part[0:16].astype(F32)
            for t in range(2):
                entries[t, :, i * 256 : i * 256 + 256] = fresh_rows[2 * t : 2 * t + 2].astype(BF)
        cps["rows"] = queries, key_now, value_now
        attention_row(0)

    def attention_row(j):
        queries, key_now, value_now = cps["rows"]
        row, col = iota((128, 256), 0), iota((128, 256), 1)
        chosen = one_hot(col == (((row >> 4) << 5) + ((row & 15) << 1) + j))
        heads = dot(chosen, queries).astype(BF)
        scores = dot_t(heads, b["keys"][j]) * (1.0 / 16.0)
        live = iota(scores.shape, 1) < lens[j]
        scores = jnp.where(live, scores, -jnp.inf)
        now = dot_t(heads, key_now) * (1.0 / 16.0)
        r, n_ = iota((128, 128), 0), iota((128, 128), 1)
        now = jnp.where((n_ < 4) & ((n_ & 1) == j) & ((n_ >> 1) <= (r & 1)), now, -jnp.inf)
        top = jnp.maximum(
            jnp.max(scores, axis=1, keepdims=True), jnp.max(now, axis=1, keepdims=True)
        )
        scores = jnp.exp(scores - top)
        now = jnp.exp(now - top)
        under = jnp.sum(scores, axis=1, keepdims=True) + jnp.sum(now, axis=1, keepdims=True)
        scale = 1.0 / under
        mixed = dot((scores * scale).astype(BF), b["values"][j]) + dot(
            (now * scale).astype(BF), value_now
        )
        brow, bcol = iota((256, 128), 0), iota((256, 128), 1)
        back = one_hot(brow == (((bcol >> 4) << 5) + ((bcol & 15) << 1) + j))
        term = dot(back, mixed.astype(BF))
        if j == 0:
            cps["term"] = term
            return
        result = cps["term"] + term
        b["asend"][...] = result.astype(BF).reshape(8, 32, 256)
        cps["a"] = exchange(b["asend"], b["arecv"])

    def attended():
        cps["a"].wait()
        raw = b["arecv"][...].reshape(256, 256)
        for f in range(2):
            h = halves[f]
            for i in range(3):
                value = dot(collect_rows(f * 3 + i), raw).astype(BF)
                b["ag", 0, f][h.p2, h.p1, :, i * 256 : i * 256 + 256] = value

    def final_order():
        row, col = iota((512, 512), 0), iota((512, 512), 1)
        gx = (((row >> 6) & 3) << 1) | (row >> 8)
        wanted = ((row >> 1) & 15) << 5 | (position(gx) << 2) | (((row >> 5) & 1) << 1) | (row & 1)
        order[0] = one_hot(wanted == col)

    stages = {
        "query_out": lambda k, f: query_out(),
        "attention": lambda k, f: attention_row(1) if k else attention(),
        "attended": lambda k, f: attended(),
        "turns": lambda k, f: turns(),
        "final_order": lambda k, f: final_order(),
        "more_loads": lambda k, f: more_loads(),
    }
    for stage in (product, s1, s2, s3, s4, hidden, g1, g2, g3, g4, second, second_early, second_late):
        stages[stage.__name__] = stage

    ordered(1, 0)
    product_group(1, 0)
    s1_group(1, 0)
    forward_l.wait()
    cross(block(zo), 1, far)
    forward_r.wait()
    cross(block(zo), 0, far)
    ordered(0, 0)
    product_group(0, 0)
    s1_group(0, 0)
    far.wait()
    for f in (1, 0):
        ordered(f, 1)
        product_group(f, 1)
        s1_group(f, 1)
    for name, k, f in ORDER:
        stages[name](k, f)

    ob, fr, fz1, fz2 = b["ob"], b["fr"], b["fz1"], b["fz2"]
    spans = (slice(0, 384), slice(384, columns))
    top, low = slice(0, 32), slice(32, 64)
    crossed = []
    for span in spans:
        rows = b["acc"][:, :, span].reshape(512, -1).astype(BF)
        ob[:, :, :, span] = dot(order[0], rows).astype(BF).reshape(2, 4, 64, -1)
        flight = Flight(fr.at[:, :, span])
        rc(ob.at[1 - c, :, :, span], fr.at[:, :, span], partner, flight, leaving(fr.at[:, :, span]))
        crossed.append(flight)
    waves = []
    for i, span in enumerate(spans):
        crossed[i].wait()

        def add_partner(zz):
            ob[c, zz, :, span] = add_f32(ob[c, zz, :, span], fr[zz, :, span]).astype(BF)

        one, two = Flight(fz1.at[:, :, span]), Flight(fz2.at[:, :, span])
        at = leaving(fr.at[0:3, :, span])
        add_partner(zo)
        rc(ob.at[c, zo, top, span], fz1.at[0, :, span], at_z(1), one, at)
        rc(ob.at[c, zo, low, span], fz1.at[1, :, span], at_z(-1), one, at)
        add_partner(zr)
        rc(ob.at[c, zr, low, span], fz2.at[0, low, span], at_z(1), two, at)
        add_partner(zl)
        rc(ob.at[c, zl, top, span], fz2.at[1, top, span], at_z(-1), two, at)
        waves.append((one, two, at))
    for i, span in enumerate(spans):
        one, two, at = waves[i]
        one.wait()
        ob[c, zr, top, span] = add_f32(ob[c, zr, top, span], fz1[0, :, span]).astype(BF)
        rc(ob.at[c, zr, top, span], fz2.at[0, top, span], at_z(1), two, at)
        ob[c, zl, low, span] = add_f32(ob[c, zl, low, span], fz1[1, :, span]).astype(BF)
        rc(ob.at[c, zl, low, span], fz2.at[1, low, span], at_z(-1), two, at)
    for i, span in enumerate(spans):
        own = add_f32(ob[c, z, :, span], fr[z, :, span])
        waves[i][1].wait()
        own = own + fz2[0, :, span].astype(F32) + fz2[1, :, span].astype(F32)
        out[:, :, span] = own.reshape(2, 32, -1)
    for ref, at in sends:
        pltpu.make_async_copy(ref, ref, send_sem.at[at]).wait()
    assert counts == {"send": SENDS, "recv": RECVS, "load": LOADS}, counts


def local(
    tokens,
    norm_gain,
    w_query,
    w_shared,
    w_gate,
    w_up,
    w_out,
    w_down,
    key_cache,
    value_cache,
    lengths,
):
    steps, block_rows, columns = tokens.shape
    model_width = columns * lax.axis_size("yz")
    frequency = np.exp(np.arange(128, dtype=np.float32) * np.float32(-2.0 * math.log(10000.0) / 256))
    plan = scratch_plan(columns)
    hbm = pl.BlockSpec(memory_space=pl.ANY)
    vmem = pl.BlockSpec(memory_space=pltpu.VMEM)
    smem = pl.BlockSpec(memory_space=pltpu.SMEM)
    layer, entries = pl.pallas_call(
        functools.partial(kernel, plan.names, model_width),
        out_shape=(
            jax.ShapeDtypeStruct((steps, block_rows, columns), F32),
            jax.ShapeDtypeStruct((2, 2, 512), BF),
        ),
        in_specs=[hbm, vmem] + [hbm] * 8 + [smem, vmem],
        out_specs=(vmem, vmem),
        scratch_shapes=plan.shapes
        + [
            pltpu.SemaphoreType.DMA((SENDS,)),
            pltpu.SemaphoreType.DMA((RECVS,)),
            pltpu.SemaphoreType.DMA((LOADS,)),
        ],
        compiler_params=pltpu.CompilerParams(
            collective_id=0, has_side_effects=True, vmem_limit_bytes=64 << 20
        ),
        cost_estimate=pl.CostEstimate(
            flops=12 * 10**9, bytes_accessed=28 * 10**6, transcendentals=10**6
        ),
    )(
        tokens.reshape(steps * block_rows, columns),
        norm_gain,
        w_query,
        w_shared,
        w_gate,
        w_up,
        w_out,
        w_down,
        key_cache,
        value_cache,
        lengths,
        jnp.asarray(frequency[None]),
    )
    return (tokens.astype(F32) + layer).astype(BF), entries


def solution(mesh):
    in_specs = (
        P(None, "gx", "yz"),
        P("yz"),
        P("yz", "gx"),
        P("yz", None),
        P("yz", "gx"),
        P("yz", "gx"),
        P("gx", "yz"),
        P("gx", "yz"),
        P(("gx", "yz"), None, None),
        P(("gx", "yz"), None, None),
        P(("gx", "yz")),
    )
    out_specs = (P(None, "gx", "yz"), P(None, ("gx", "yz"), None))
    return jax.shard_map(local, mesh=mesh, in_specs=in_specs, out_specs=out_specs, check_vma=False)
```

```python
import functools
import math

import jax
import jax.numpy as jnp
import numpy as np
from jax import lax
from jax.experimental import pallas as pl
from jax.experimental.pallas import tpu as pltpu
from jax.sharding import PartitionSpec as P

EPSILON = 1e-06
MESH = pl.DeviceIdType.MESH
BF = jnp.bfloat16
F32 = jnp.float32
HIDDEN_CHUNKS = (768, 768, 768)
RING = 4
ORDER = (
    ("more_loads", 0, 0),
    ("product", 1, 0),
    ("s2", 0, 1),
    ("s1", 1, 0),
    ("product", 1, 1),
    ("s1", 1, 1),
    ("s3", 0, 1),
    ("product", 2, 1),
    ("product", 3, 1),
    ("s2", 1, 1),
    ("s2", 0, 0),
    ("s2", 1, 0),
    ("final_order", 0, 0),
    ("product", 3, 0),
    ("s3", 0, 0),
    ("s1", 3, 0),
    ("s1", 2, 1),
    ("s4", 0, 1),
    ("s4", 0, 0),
    ("turns", 0, 0),
    ("product", 2, 0),
    ("s1", 2, 0),
    ("s1", 3, 1),
    ("s3", 1, 1),
    ("query_out", 0, 0),
    ("s2", 2, 1),
    ("s2", 2, 0),
    ("attention", 0, 0),
    ("s2", 3, 0),
    ("s3", 1, 0),
    ("s2", 3, 1),
    ("attention", 1, 0),
    ("s4", 1, 0),
    ("s3", 2, 0),
    ("s3", 2, 1),
    ("s4", 1, 1),
    ("s3", 3, 0),
    ("hidden", 1, 0),
    ("s4", 2, 1),
    ("attended", 0, 0),
    ("g1", 0, 1),
    ("g1", 0, 0),
    ("g1", 1, 0),
    ("s3", 3, 1),
    ("hidden", 1, 1),
    ("s4", 2, 0),
    ("g1", 1, 1),
    ("g2", 0, 1),
    ("s4", 3, 0),
    ("g2", 0, 0),
    ("hidden", 2, 1),
    ("s4", 3, 1),
    ("g1", 2, 1),
    ("g2", 1, 1),
    ("hidden", 2, 0),
    ("g1", 2, 0),
    ("g3", 0, 0),
    ("g2", 1, 0),
    ("hidden", 3, 0),
    ("hidden", 3, 1),
    ("g1", 3, 1),
    ("g3", 0, 1),
    ("g3", 1, 1),
    ("g3", 1, 0),
    ("g1", 3, 0),
    ("g2", 3, 1),
    ("g2", 2, 0),
    ("g2", 2, 1),
    ("g4", 0, 0),
    ("g4", 0, 1),
    ("g2", 3, 0),
    ("g3", 2, 0),
    ("g3", 2, 1),
    ("second", 0, 0),
    ("g4", 1, 0),
    ("g4", 1, 1),
    ("g3", 3, 0),
    ("g4", 2, 0),
    ("g3", 3, 1),
    ("second", 1, 0),
    ("g4", 2, 1),
    ("second", 1, 1),
    ("g4", 3, 1),
    ("g4", 3, 0),
    ("second", 0, 1),
    ("second", 2, 0),
    ("second", 2, 1),
    ("second_early", 3, 0),
    ("second_early", 3, 1),
    ("second_late", 3, 0),
    ("second_late", 3, 1),
)
SENDS, RECVS, LOADS = 39, 80, 19


def dot(a, b):
    return jnp.dot(a, b, preferred_element_type=F32)


def dot_t(a, b):
    return lax.dot_general(a, b, (((1,), (1,)), ((), ())), preferred_element_type=F32)


def iota(shape, dim):
    return lax.broadcasted_iota(jnp.int32, shape, dim)


def one_hot(mask):
    return jnp.where(mask, 1.0, 0.0).astype(BF)


def add_f32(*terms):
    total = terms[0].astype(F32)
    for term in terms[1:]:
        total = total + term.astype(F32)
    return total


class Scratch:
    def __init__(self):
        self.names, self.shapes = [], []

    def add(self, name, shape, dtype=BF):
        self.names.append(name)
        self.shapes.append(pltpu.VMEM(shape, dtype))


def query_width(f):
    return 768 + 128 * f


def scratch_plan(columns):
    s = Scratch()
    for f in range(2):
        for k in range(1 + len(HIDDEN_CHUNKS)):
            hc = 768 if k == 0 else HIDDEN_CHUNKS[k - 1]
            w = query_width(f) if k == 0 else 2 * hc
            t = (k, f)
            s.add(("w1",) + t, (columns, w))
            s.add(("part",) + t, (4, 4, 32, w))
            s.add(("r1",) + t, (2, 2, 32, w))
            s.add(("r2",) + t, (2, 4, 32, w))
            s.add(("q1",) + t, (2, 16, w))
            s.add(("q2",) + t, (2, 32, w))
            s.add(("ag",) + t, (4, 4, 32, hc))
            s.add(("w2",) + t, (hc, columns))
    s.add("keys", (2, 2048, 256))
    s.add("values", (2, 2048, 256))
    s.add("tk", (8, 64, columns))
    s.add("order", (2, 512, 512))
    s.add("xs", (2, 2, 256, columns))
    s.add("acc", (16, 32, columns), F32)
    s.add("ob", (2, 4, 64, columns))
    s.add("fr", (4, 64, columns))
    s.add("fz1", (2, 32, columns))
    s.add("fz2", (2, 64, columns))
    s.add("qsend", (8, 32, 256))
    s.add("qrecv", (8, 32, 256))
    s.add("asend", (8, 32, 256))
    s.add("arecv", (8, 32, 256))
    s.add("inv", (32, 128), F32)
    s.add("turn", (2, 8, 128), F32)
    return s


class Half:
    pass


def kernel(
    plan_names,
    model_width,
    tok,
    gain,
    wq,
    wsh,
    wg,
    wu,
    wo,
    wd,
    kc,
    vc,
    lens,
    frequency,
    out,
    entries,
    *scratch,
):
    n = len(plan_names)
    b = dict(zip(plan_names, scratch[:n]))
    send_sem, recv_sem, local_sem = scratch[n:]
    columns = tok.shape[1]
    g = lax.axis_index("gx")
    q = lax.axis_index("yz")
    z, c = g // 2, lax.rem(g, 2)
    y, x = q // 4, lax.rem(q, 4)

    def step(v, d):
        return lax.rem(v + d + RING, RING)

    def at_x(d):
        return (g, y * 4 + step(x, d))

    def at_y(d):
        return (g, step(y, d) * 4 + x)

    def at_z(d):
        return (step(z, d) * 2 + c, q)

    partner = (z * 2 + 1 - c, q)

    sends, counts = [], {"send": 0, "recv": 0, "load": 0}

    def fresh(kind):
        counts[kind] += 1
        return counts[kind] - 1

    class Flight:
        def __init__(self, arriving):
            self.arriving, self.at = arriving, fresh("recv")

        def wait(self):
            pltpu.make_async_copy(self.arriving, self.arriving, recv_sem.at[self.at]).wait()

    def leaving(ref):
        at = fresh("send")
        sends.append((ref, at))
        return at

    def rc(src, dst, dev, flight, at):
        pltpu.make_async_remote_copy(
            src_ref=src,
            dst_ref=dst,
            send_sem=send_sem.at[at],
            recv_sem=recv_sem.at[flight.at],
            device_id=dev,
            device_id_type=MESH,
        ).start()

    loads = {}

    def load(name, whole, *pairs):
        at = fresh("load")
        for src, dst in pairs:
            pltpu.make_async_copy(src, dst, local_sem.at[at]).start()
        loads[name] = (whole, at)

    def loaded(name):
        whole, at = loads[name]
        pltpu.make_async_copy(whole, whole, local_sem.at[at]).wait()

    barrier = pltpu.get_barrier_semaphore()
    others = [lax.rem(g + d, 8) for d in range(1, 8)]
    peers = [at_x(1), at_x(-1), at_y(1), at_y(-1)] + [(o, q) for o in others]
    for peer in peers:
        pl.semaphore_signal(barrier, inc=1, device_id=peer, device_id_type=MESH)

    load("tok", b["tk"].at[g], (tok, b["tk"].at[g]))
    shared_at = pl.multiple_of(z * 128, 128)
    w1 = b["w1", 0, 1]
    load(
        ("w1", 0, 1),
        w1,
        (wq.at[:, 768:1536], w1.at[:, 0:768]),
        (wsh.at[:, pl.ds(shared_at, 128)], w1.at[:, 768:896]),
    )
    load(("w1", 0, 0), b["w1", 0, 0], (wq.at[:, 0:768], b["w1", 0, 0]))
    hidden_at = {}
    base = 0
    for k, hc in enumerate(HIDDEN_CHUNKS, 1):
        for f in range(2):
            hidden_at[k, f] = base
            base += hc

    def load_w1(k):
        hc = HIDDEN_CHUNKS[k - 1]
        for f in range(2):
            at = hidden_at[k, f]
            w1 = b["w1", k, f]
            load(
                ("w1", k, f),
                w1,
                (wg.at[:, at : at + hc], w1.at[:, 0:hc]),
                (wu.at[:, at : at + hc], w1.at[:, hc : 2 * hc]),
            )

    loaded("tok")
    pl.semaphore_wait(barrier, len(peers))

    tk = b["tk"]

    def block(zz):
        return zz * 2 + c

    zr, zl, zo = step(z, 1), step(z, -1), step(z, 2)
    parts = (pl.ds(0, 32), pl.ds(32, 32))

    token_sends = leaving(tk.at[0:7])
    near, far = Flight(tk.at[0:2]), Flight(tk.at[0:2])

    def send(blk, i, dev, flight=None):
        ref = tk.at[blk, parts[i]]
        flight = flight or Flight(ref)
        rc(ref, ref, dev, flight, token_sends)
        return flight

    def cross(blk, i, flight):
        send(blk, i, partner, flight)

    left_first = send(g, 1, at_z(-1))
    right_first = send(g, 0, at_z(1))
    left_last = send(g, 0, at_z(-1))
    right_last = send(g, 1, at_z(1))
    cross(g, 0, near)
    cross(g, 1, near)
    for k in range(1, 1 + len(HIDDEN_CHUNKS)):
        load_w1(k)
    row_i, col_i = iota((256, 256), 0), iota((256, 256), 1)
    tail = (((row_i >> 2) & 3) << 6) | (((row_i >> 1) & 1) << 5) | (row_i & 1)
    d1, d2 = (row_i >> 6) & 3, (row_i >> 4) & 3
    order = b["order"]
    order[0, 0:256, 0:256] = one_hot((tail | (d2 << 3) | (d1 << 1)) == col_i)
    order[1, 0:256, 0:256] = one_hot((tail | (d1 << 3) | (d2 << 1)) == col_i)
    left_first.wait()
    forward_l = send(block(zr), 1, at_z(-1))
    cross(block(zr), 1, near)
    right_first.wait()
    forward_r = send(block(zl), 0, at_z(1))
    left_last.wait()
    cross(block(zr), 0, near)
    cross(block(zl), 0, far)
    right_last.wait()
    cross(block(zl), 1, far)
    near.wait()

    squares = {}
    gain_row = gain[...].reshape(1, columns)

    def position(gx):
        return ((((gx >> 1) + 4 - z) & 3) << 1) | (gx & 1)

    def ordered(f, group):
        planes = [tk[pl.ds(step(z, 2 * group + i) * 2, 2)].reshape(128, columns) for i in range(2)]
        rows = dot(order[f, 0:256, 0:256], jnp.concatenate(planes, axis=0))
        if f == 1:
            squares[group] = jnp.sum(rows * rows, axis=1, keepdims=True)
        b["xs"][f, group] = (rows * gain_row).astype(BF)

    def more_loads():
        for k in range(1 + len(HIDDEN_CHUNKS)):
            for f in range(2):
                w2 = b["w2", k, f]
                if k == 0:
                    load(("w2", k, f), w2, (wo.at[768 * f : 768 * f + 768], w2))
                else:
                    at = hidden_at[k, f]
                    load(("w2", k, f), w2, (wd.at[at : at + HIDDEN_CHUNKS[k - 1]], w2))
        load("keys", b["keys"], (kc, b["keys"]))
        load("values", b["values"], (vc, b["values"]))

    lane = iota((1, 128), 1)
    mine = (lane >> 6) == c
    spread = 1.0 + (lane & 63).astype(F32) * (1.0 / 64.0)

    halves = {}
    for f in range(2):
        h = Half()
        first, second = (at_x, at_y) if f == 0 else (at_y, at_x)
        p1, p2 = (x, y) if f == 0 else (y, x)
        h.first, h.second, h.p1, h.p2 = first, second, p1, p2
        h.r1, h.l1, h.o1 = step(p1, 1), step(p1, -1), step(p1, 2)
        h.r2, h.l2, h.o2 = step(p2, 1), step(p2, -1), step(p2, 2)
        halves[f] = h
    cps = {}

    def product(k, f):
        loaded(("w1", k, f))
        part, w1, xs = b["part", k, f], b["w1", k, f], b["xs"]

        @pl.loop(0, w1.shape[1] // 256)
        def _(i):
            at = pl.ds(pl.multiple_of(i * 256, 256), 256)
            value = dot(xs[f].reshape(512, columns), w1[:, at]).astype(BF)
            value = value.reshape(2, 4, 4, 16, 256)
            part[:, :, 0:16, at] = value[0]
            part[:, :, 16:32, at] = value[1]

    def product_group(f, group):
        if group == 0:
            loaded(("w1", 0, f))
        part, w1, xs = b["part", 0, f], b["w1", 0, f], b["xs"]
        lines = slice(16 * group, 16 * group + 16)
        for i in range(3):
            at = slice(i * 256, i * 256 + 256)
            value = dot(xs[f, group], w1[:, at]).astype(BF)
            part[:, :, lines, at] = value.reshape(4, 4, 16, 256)
        if f == 1:
            value = dot(xs[f, group], w1[:, 768:896])
            value = jnp.where(mine, value, squares[group] * spread).astype(BF)
            part[:, :, lines, 768:896] = value.reshape(4, 4, 16, 128)

    def s1_group(f, group):
        h, part, r1, r2 = halves[f], b["part", 0, f], b["r1", 0, f], b["r2", 0, f]
        if group == 0:
            cps[0, f] = Flight(r1), Flight(r2), leaving(part.at[0:3])
        one, two, at = cps[0, f]
        lines = slice(16 * group, 16 * group + 16)
        rc(part.at[h.o1, 0:2, lines], r1.at[0, :, lines], h.first(1), one, at)
        rc(part.at[h.o1, 2:4, lines], r1.at[1, :, lines], h.first(-1), one, at)
        rc(part.at[h.r1, 2:4, lines], r2.at[0, 2:4, lines], h.first(1), two, at)
        rc(part.at[h.l1, 0:2, lines], r2.at[1, 0:2, lines], h.first(-1), two, at)

    def s1(k, f):
        h, part, r1, r2 = halves[f], b["part", k, f], b["r1", k, f], b["r2", k, f]
        one, two, at = Flight(r1), Flight(r2), leaving(part.at[0:3])
        rc(part.at[h.o1, 0:2], r1.at[0], h.first(1), one, at)
        rc(part.at[h.o1, 2:4], r1.at[1], h.first(-1), one, at)
        rc(part.at[h.r1, 2:4], r2.at[0, 2:4], h.first(1), two, at)
        rc(part.at[h.l1, 0:2], r2.at[1, 0:2], h.first(-1), two, at)
        cps[k, f] = one, two, at

    def s2(k, f):
        h, part, r1, r2 = halves[f], b["part", k, f], b["r1", k, f], b["r2", k, f]
        one, two, at = cps[k, f]
        one.wait()
        part[h.r1, 0:2] = add_f32(part[h.r1, 0:2], r1[0]).astype(BF)
        rc(part.at[h.r1, 0:2], r2.at[0, 0:2], h.first(1), two, at)
        part[h.l1, 2:4] = add_f32(part[h.l1, 2:4], r1[1]).astype(BF)
        rc(part.at[h.l1, 2:4], r2.at[1, 2:4], h.first(-1), two, at)

    def s3(k, f):
        h, part, r2 = halves[f], b["part", k, f], b["r2", k, f]
        q1, q2 = b["q1", k, f], b["q2", k, f]
        cps[k, f][1].wait()

        def total(d):
            part[h.p1, d] = add_f32(part[h.p1, d], r2[0, d], r2[1, d]).astype(BF)

        one, two, at = Flight(q1), Flight(q2), leaving(part.at[0, 0:3])
        total(h.o2)
        rc(part.at[h.p1, h.o2, 0:16], q1.at[0], h.second(1), one, at)
        rc(part.at[h.p1, h.o2, 16:32], q1.at[1], h.second(-1), one, at)
        total(h.r2)
        rc(part.at[h.p1, h.r2, 16:32], q2.at[0, 16:32], h.second(1), two, at)
        total(h.l2)
        rc(part.at[h.p1, h.l2, 0:16], q2.at[1, 0:16], h.second(-1), two, at)
        total(h.p2)
        cps[k, f] = one, two, at

    def s4(k, f):
        h, part = halves[f], b["part", k, f]
        q1, q2 = b["q1", k, f], b["q2", k, f]
        one, two, at = cps[k, f]
        one.wait()
        part[h.p1, h.r2, 0:16] = add_f32(part[h.p1, h.r2, 0:16], q1[0]).astype(BF)
        rc(part.at[h.p1, h.r2, 0:16], q2.at[0, 0:16], h.second(1), two, at)
        part[h.p1, h.l2, 16:32] = add_f32(part[h.p1, h.l2, 16:32], q1[1]).astype(BF)
        rc(part.at[h.p1, h.l2, 16:32], q2.at[1, 16:32], h.second(-1), two, at)

    def s5(k, f, lo, hi):
        h, part, q2 = halves[f], b["part", k, f], b["q2", k, f]
        return add_f32(part[h.p1, h.p2, :, lo:hi], q2[0, :, lo:hi], q2[1, :, lo:hi])

    def s5_wait(k, f):
        cps[k, f][1].wait()

    def hidden(k, f):
        s5_wait(k, f)
        h, hc = halves[f], HIDDEN_CHUNKS[k - 1]
        inv = b["inv"][:, 0:1]
        gate = s5(k, f, 0, hc) * inv
        up = s5(k, f, hc, 2 * hc) * inv
        value = gate * (1.0 / (1.0 + jnp.exp(-gate))) * up
        b["ag", k, f][h.p2, h.p1] = value.astype(BF)

    def g1(k, f):
        h, ag = halves[f], b["ag", k, f]
        one, two, at = Flight(ag.at[0, 0:2]), Flight(ag.at[0, 0]), leaving(ag.at[0, 0:3])
        blk = ag.at[h.p2, h.p1]
        rc(blk, blk, h.first(1), one, at)
        rc(blk, blk, h.first(-1), one, at)
        cps["g", k, f] = one, two, at

    def g2(k, f):
        h, ag = halves[f], b["ag", k, f]
        one, two, at = cps["g", k, f]
        one.wait()
        blk = ag.at[h.p2, h.l1, 0:16]
        rc(blk, blk, h.first(1), two, at)
        blk = ag.at[h.p2, h.r1, 16:32]
        rc(blk, blk, h.first(-1), two, at)

    def g3(k, f):
        h, ag = halves[f], b["ag", k, f]
        cps["g", k, f][1].wait()
        one, two, at = Flight(ag.at[0:2]), Flight(ag.at[0]), leaving(ag.at[0:3])
        blk = ag.at[h.p2]
        rc(blk, blk, h.second(1), one, at)
        rc(blk, blk, h.second(-1), one, at)
        cps["g", k, f] = one, two, at

    def g4(k, f):
        h, ag = halves[f], b["ag", k, f]
        one, two, at = cps["g", k, f]
        one.wait()
        blk = ag.at[h.l2, 0:2]
        rc(blk, blk, h.second(1), two, at)
        blk = ag.at[h.r2, 2:4]
        rc(blk, blk, h.second(-1), two, at)

    first_product = [True]

    def second(k, f):
        cps["g", k, f][1].wait()
        loaded(("w2", k, f))
        ag, w2, acc = b["ag", k, f], b["w2", k, f], b["acc"]
        start = first_product[0]
        first_product[0] = False
        for lo, hi in ((0, 256), (256, 512), (512, columns)):
            value = dot(ag[...].reshape(512, ag.shape[3]), w2[:, lo:hi])
            value = value.reshape(16, 32, hi - lo)
            for i in range(16):
                to = i if f == 0 else i % 4 * 4 + i // 4
                if start:
                    acc[to, :, lo:hi] = value[i]
                else:
                    acc[to, :, lo:hi] += value[i]

    def second_rows(k, f, d):
        ag, w2, acc = b["ag", k, f], b["w2", k, f], b["acc"]
        value = dot(ag[d].reshape(128, ag.shape[3]), w2[...]).reshape(4, 32, columns)
        for i in range(4):
            at = d * 4 + i if f == 0 else i * 4 + d
            acc[at] += value[i]

    def second_early(k, f):
        h = halves[f]
        loaded(("w2", k, f))
        for d in (h.p2, h.l2, h.r2):
            second_rows(k, f, d)

    def second_late(k, f):
        cps["g", k, f][1].wait()
        second_rows(k, f, halves[f].o2)

    def exchange(send, recv):
        flight, at = Flight(recv.at[0:7]), leaving(send.at[0:7])
        for o in others:
            rc(send.at[o], recv.at[g], (o, q), flight, at)
        recv[g] = send[g]
        return flight

    def spread_rows(head):
        row, col = iota((256, 32), 0), iota((256, 32), 1)
        return one_hot((col == ((position(row >> 5) << 2) | (row & 3))) & (((row >> 2) & 7) == head))

    def collect_rows(head):
        row, col = iota((32, 256), 0), iota((32, 256), 1)
        return one_hot((row == ((position(col >> 5) << 2) | (col & 3))) & (((col >> 2) & 7) == head))

    def query_out():
        s5_wait(0, 0)
        s5_wait(0, 1)
        shared = s5(0, 1, 768, 896)
        total = jnp.sum(jnp.where(mine, 0.0, shared), axis=1, keepdims=True) * (1.0 / 95.5)
        inv = lax.rsqrt(total / model_width + EPSILON)
        b["inv"][...] = jnp.broadcast_to(inv, (32, 128))
        shared = jnp.where(mine, shared * inv, 0.0)
        low = lax.rem(z, 2) == 0
        shared = jnp.concatenate([jnp.where(low, shared, 0.0), jnp.where(low, 0.0, shared)], axis=1)
        rows = dot(spread_rows(6), shared.astype(BF))
        for f in range(2):
            for i in range(3):
                piece = (s5(0, f, i * 256, i * 256 + 256) * inv).astype(BF)
                rows = rows + dot(spread_rows(f * 3 + i), piece)
        b["qsend"][...] = rows.astype(BF).reshape(8, 32, 256)
        cps["q"] = exchange(b["qsend"], b["qrecv"])

    def rotate(rows):
        count = rows.shape[0]
        rows = rows.reshape(count // 8, 8, 256)
        front, back = rows[:, :, :128], rows[:, :, 128:]
        cosine, sine = b["turn"][0][None], b["turn"][1][None]
        return jnp.concatenate(
            [front * cosine - back * sine, back * cosine + front * sine], axis=2
        ).reshape(count, 256)

    def turns():
        row = iota((8, 128), 0)
        position = jnp.where((row & 1) == 0, lens[0], lens[1]) + ((row >> 1) & 1)
        angles = position.astype(F32) * frequency[...]
        b["turn"][0] = jnp.cos(angles)
        b["turn"][1] = jnp.sin(angles)

    def attention():
        cps["q"].wait()
        loaded("keys")
        loaded("values")
        raw = b["qrecv"][...].reshape(256, 256)
        queries = rotate(raw.astype(F32)).astype(BF)
        row, col = iota((128, 256), 0), iota((128, 256), 1)
        pick = (row < 4) & ((col & 31) == row + 24)
        key_now = rotate(dot(one_hot(pick & (col < 128)), raw)).astype(BF)
        value_now = dot(one_hot(pick & (col >= 128)), raw).astype(BF)
        for i, part in enumerate((key_now, value_now)):
            fresh_rows = part[0:16].astype(F32)
            for t in range(2):
                entries[t, :, i * 256 : i * 256 + 256] = fresh_rows[2 * t : 2 * t + 2].astype(BF)
        cps["rows"] = queries, key_now, value_now
        attention_row(0)

    def attention_row(j):
        queries, key_now, value_now = cps["rows"]
        row, col = iota((128, 256), 0), iota((128, 256), 1)
        chosen = one_hot(col == (((row >> 4) << 5) + ((row & 15) << 1) + j))
        heads = dot(chosen, queries).astype(BF)
        scores = dot_t(heads, b["keys"][j]) * (1.0 / 16.0)
        live = iota(scores.shape, 1) < lens[j]
        scores = jnp.where(live, scores, -jnp.inf)
        now = dot_t(heads, key_now) * (1.0 / 16.0)
        r, n_ = iota((128, 128), 0), iota((128, 128), 1)
        now = jnp.where((n_ < 4) & ((n_ & 1) == j) & ((n_ >> 1) <= (r & 1)), now, -jnp.inf)
        top = jnp.maximum(
            jnp.max(scores, axis=1, keepdims=True), jnp.max(now, axis=1, keepdims=True)
        )
        scores = jnp.exp(scores - top)
        now = jnp.exp(now - top)
        under = jnp.sum(scores, axis=1, keepdims=True) + jnp.sum(now, axis=1, keepdims=True)
        scale = 1.0 / under
        mixed = dot((scores * scale).astype(BF), b["values"][j]) + dot(
            (now * scale).astype(BF), value_now
        )
        brow, bcol = iota((256, 128), 0), iota((256, 128), 1)
        back = one_hot(brow == (((bcol >> 4) << 5) + ((bcol & 15) << 1) + j))
        term = dot(back, mixed.astype(BF))
        if j == 0:
            cps["term"] = term
            return
        result = cps["term"] + term
        b["asend"][...] = result.astype(BF).reshape(8, 32, 256)
        cps["a"] = exchange(b["asend"], b["arecv"])

    def attended():
        cps["a"].wait()
        raw = b["arecv"][...].reshape(256, 256)
        for f in range(2):
            h = halves[f]
            for i in range(3):
                value = dot(collect_rows(f * 3 + i), raw).astype(BF)
                b["ag", 0, f][h.p2, h.p1, :, i * 256 : i * 256 + 256] = value

    def final_order():
        row, col = iota((512, 512), 0), iota((512, 512), 1)
        gx = (((row >> 6) & 3) << 1) | (row >> 8)
        wanted = ((row >> 1) & 15) << 5 | (position(gx) << 2) | (((row >> 5) & 1) << 1) | (row & 1)
        order[0] = one_hot(wanted == col)

    stages = {
        "query_out": lambda k, f: query_out(),
        "attention": lambda k, f: attention_row(1) if k else attention(),
        "attended": lambda k, f: attended(),
        "turns": lambda k, f: turns(),
        "final_order": lambda k, f: final_order(),
        "more_loads": lambda k, f: more_loads(),
    }
    for stage in (product, s1, s2, s3, s4, hidden, g1, g2, g3, g4, second, second_early, second_late):
        stages[stage.__name__] = stage

    ordered(1, 0)
    product_group(1, 0)
    s1_group(1, 0)
    forward_l.wait()
    cross(block(zo), 1, far)
    forward_r.wait()
    cross(block(zo), 0, far)
    ordered(0, 0)
    product_group(0, 0)
    s1_group(0, 0)
    far.wait()
    for f in (1, 0):
        ordered(f, 1)
        product_group(f, 1)
        s1_group(f, 1)
    for name, k, f in ORDER:
        stages[name](k, f)

    ob, fr, fz1, fz2 = b["ob"], b["fr"], b["fz1"], b["fz2"]
    spans = (slice(0, 384), slice(384, columns))
    top, low = slice(0, 32), slice(32, 64)
    crossed = []
    for span in spans:
        rows = b["acc"][:, :, span].reshape(512, -1).astype(BF)
        ob[:, :, :, span] = dot(order[0], rows).astype(BF).reshape(2, 4, 64, -1)
        flight = Flight(fr.at[:, :, span])
        rc(ob.at[1 - c, :, :, span], fr.at[:, :, span], partner, flight, leaving(fr.at[:, :, span]))
        crossed.append(flight)
    waves = []
    for i, span in enumerate(spans):
        crossed[i].wait()

        def add_partner(zz):
            ob[c, zz, :, span] = add_f32(ob[c, zz, :, span], fr[zz, :, span]).astype(BF)

        one, two = Flight(fz1.at[:, :, span]), Flight(fz2.at[:, :, span])
        at = leaving(fr.at[0:3, :, span])
        add_partner(zo)
        rc(ob.at[c, zo, top, span], fz1.at[0, :, span], at_z(1), one, at)
        rc(ob.at[c, zo, low, span], fz1.at[1, :, span], at_z(-1), one, at)
        add_partner(zr)
        rc(ob.at[c, zr, low, span], fz2.at[0, low, span], at_z(1), two, at)
        add_partner(zl)
        rc(ob.at[c, zl, top, span], fz2.at[1, top, span], at_z(-1), two, at)
        waves.append((one, two, at))
    for i, span in enumerate(spans):
        one, two, at = waves[i]
        one.wait()
        ob[c, zr, top, span] = add_f32(ob[c, zr, top, span], fz1[0, :, span]).astype(BF)
        rc(ob.at[c, zr, top, span], fz2.at[0, top, span], at_z(1), two, at)
        ob[c, zl, low, span] = add_f32(ob[c, zl, low, span], fz1[1, :, span]).astype(BF)
        rc(ob.at[c, zl, low, span], fz2.at[1, low, span], at_z(-1), two, at)
    for i, span in enumerate(spans):
        own = add_f32(ob[c, z, :, span], fr[z, :, span])
        waves[i][1].wait()
        own = own + fz2[0, :, span].astype(F32) + fz2[1, :, span].astype(F32)
        out[:, :, span] = own.reshape(2, 32, -1)
    for ref, at in sends:
        pltpu.make_async_copy(ref, ref, send_sem.at[at]).wait()
    assert counts == {"send": SENDS, "recv": RECVS, "load": LOADS}, counts


def local(
    tokens,
    norm_gain,
    w_query,
    w_shared,
    w_gate,
    w_up,
    w_out,
    w_down,
    key_cache,
    value_cache,
    lengths,
):
    steps, block_rows, columns = tokens.shape
    model_width = columns * lax.axis_size("yz")
    frequency = np.exp(np.arange(128, dtype=np.float32) * np.float32(-2.0 * math.log(10000.0) / 256))
    plan = scratch_plan(columns)
    hbm = pl.BlockSpec(memory_space=pl.ANY)
    vmem = pl.BlockSpec(memory_space=pltpu.VMEM)
    smem = pl.BlockSpec(memory_space=pltpu.SMEM)
    layer, entries = pl.pallas_call(
        functools.partial(kernel, plan.names, model_width),
        out_shape=(
            jax.ShapeDtypeStruct((steps, block_rows, columns), F32),
            jax.ShapeDtypeStruct((2, 2, 512), BF),
        ),
        in_specs=[hbm, vmem] + [hbm] * 8 + [smem, vmem],
        out_specs=(vmem, vmem),
        scratch_shapes=plan.shapes
        + [
            pltpu.SemaphoreType.DMA((SENDS,)),
            pltpu.SemaphoreType.DMA((RECVS,)),
            pltpu.SemaphoreType.DMA((LOADS,)),
        ],
        compiler_params=pltpu.CompilerParams(
            collective_id=0, has_side_effects=True, vmem_limit_bytes=64 << 20
        ),
        cost_estimate=pl.CostEstimate(
            flops=12 * 10**9, bytes_accessed=28 * 10**6, transcendentals=10**6
        ),
    )(
        tokens.reshape(steps * block_rows, columns),
        norm_gain,
        w_query,
        w_shared,
        w_gate,
        w_up,
        w_out,
        w_down,
        key_cache,
        value_cache,
        lengths,
        jnp.asarray(frequency[None]),
    )
    return (tokens.astype(F32) + layer).astype(BF), entries


def solution(mesh):
    in_specs = (
        P(None, "gx", "yz"),
        P("yz"),
        P("yz", "gx"),
        P("yz", None),
        P("yz", "gx"),
        P("yz", "gx"),
        P("gx", "yz"),
        P("gx", "yz"),
        P(("gx", "yz"), None, None),
        P(("gx", "yz"), None, None),
        P(("gx", "yz")),
    )
    out_specs = (P(None, "gx", "yz"), P(None, ("gx", "yz"), None))
    return jax.shard_map(local, mesh=mesh, in_specs=in_specs, out_specs=out_specs, check_vma=False)
```
